32 devices in a mesh: rows: 8 (over z, x), blk: 4 (over y, core).
Axes of the slice: x: 2, y: 2, z: 4, core: 2. Of those that a mesh axis runs over, the one named last changes fastest.
Arguments:
- block_weight: bfloat16 [8, 4, 4, 64, 128, 128], P('rows', 'blk'), may hold values from 0.049804688 to 50
- block_row: int32 [8, 4, 4, 64], P('rows', 'blk'), may hold values from 0 to 15, as said below
- block_col: int32 [8, 4, 4, 64], P('rows', 'blk'), may hold values from 0 to 7, as said below
- block_count: int32 [8, 4, 4], P('rows', 'blk'), may hold values from 1 to 64, as said below
- block_samples: int32 [8, 4, 4, 64], P('rows', 'blk'), may hold values from 1 to 8
- row_degree: float32 [8, 4, 2048], P('rows', 'blk'), may hold values from 0.125 to 8
- col_degree: float32 [4, 1024], P('blk', 'rows'), may hold values from 1 to 8
- test_matrix: bfloat16 [4, 1024, 128], P('blk', 'rows'), may hold values from -6 to 6
Outputs:
- basis: float32 [8, 4, 2048, 128], P('rows', 'blk')
- triangle: float32 [128, 128], replicated
The draws below stay inside these ranges and needn't reach their ends.
Inputs may be any that keep to these rules, and one draw needn't show every extreme that they name: Within one band and slab, the slots k < 64 hold distinct (block_row, block_col) pairs. `block_col`: see block_row: pairs are distinct within one band and slab. `block_count`: some band and slab has all 64 slots live in every draw.
All inputs are finite; a program needn't handle non-finite values.
Results may differ from the reference program's by a relative error of at most 0.0065.
Values may be sent and summed in bfloat16 or wider, within the bound.
No kernel may reach another device: no remote copies, remote signals or barrier semaphores. Data moves between devices by JAX's collectives and lax.ppermute only.
A program may use at most 64 MiB of HBM per device.

```python
import math
import jax
import jax.numpy as jnp
from jax import lax

BLK = 128
SKETCH = 128
RB_DEV = 16
SLAB_BLK = 8
CAP = 64
BAND = 2048
SLAB = 1024
N_ROWS = 8
N_BLK = 4


def coord_pairs(key):
    keys = jax.random.split(jax.random.fold_in(key, 11), N_ROWS * N_BLK * N_BLK)
    perms = jax.vmap(lambda k: jax.random.permutation(k, RB_DEV * SLAB_BLK)[:CAP])(keys)
    return perms.reshape(N_ROWS, N_BLK, N_BLK, CAP).astype(jnp.int32)


def draw_block_row(key, part):
    return coord_pairs(key) // SLAB_BLK


def draw_block_col(key, part):
    return coord_pairs(key) % SLAB_BLK


def draw_block_count(key, part):
    base = jax.random.randint(jax.random.fold_in(key, 5), (N_ROWS * N_BLK * N_BLK,), CAP // 4, CAP + 1)
    where = jax.random.randint(jax.random.fold_in(key, 6), (), 0, N_ROWS * N_BLK * N_BLK)
    base = base.at[where].set(CAP)
    return jnp.maximum(base, 1).reshape(N_ROWS, N_BLK, N_BLK).astype(jnp.int32)


def draw_row_degree(key, part):
    shape = (N_ROWS, N_BLK, BAND)
    base_deg = jnp.exp(jax.random.uniform(jax.random.fold_in(key, 22), shape, jnp.float32, 0.0, jnp.log(8.0)))
    band_total = N_ROWS * N_BLK
    band_place = jnp.arange(band_total, dtype=jnp.float32).reshape(N_ROWS, N_BLK, 1) / max(band_total - 1, 1)
    factor = jnp.exp2(-3.0 * band_place)
    return (base_deg * factor).astype(jnp.float32)


def place_ends(drawn, rng, least, largest):
    index_at = [jax.random.randint(jax.random.fold_in(rng, axis), (), 0, length) for axis, length in enumerate(drawn.shape)]
    longest = drawn.shape.index(max(drawn.shape))
    next_to = index_at[:longest] + [(index_at[longest] + 1) % drawn.shape[longest]] + index_at[longest + 1:]
    return drawn.at[tuple(index_at)].set(least).at[tuple(next_to)].set(largest)


def level_of(rng, shape, cuts, low, top_value):
    gain = 1.0
    for axis_at, parts in cuts:
        draws = jax.random.uniform(jax.random.fold_in(jax.random.fold_in(rng, 6), axis_at), (parts,), jnp.float32, low / len(cuts), top_value / len(cuts))
        gain = gain * jnp.repeat(jnp.exp(draws), shape[axis_at] // parts).reshape((-1,) + (1,) * (len(shape) - 1 - axis_at))
    return gain


def noise(rng, extent, deviation, limit, cuts=(), kind=jnp.bfloat16):
    factor_of = level_of(rng, extent, cuts, -0.22, 0.18) if cuts else 1.0
    values = jax.random.normal(rng, extent, jnp.float32) * deviation * factor_of
    return jnp.minimum(jnp.maximum(values, -limit), limit).astype(kind)


def setup_inputs(seed: int = 0) -> dict:
    streams_of = jax.random.split(jax.random.key(seed), 9)
    return {
        "block_weight": jnp.clip(jnp.exp(math.log(50.0) - 6.9116692 * jax.random.uniform(streams_of[0], (N_ROWS, N_BLK, N_BLK, CAP, BLK, BLK), jnp.float32) ** level_of(streams_of[0], (N_ROWS, N_BLK, N_BLK, CAP, BLK, BLK), ((0, 8), (1, 4)), -0.2, 0.2)), 0.049804688, 50.0).astype(jnp.bfloat16),
        "block_row": draw_block_row(jax.random.fold_in(streams_of[8], 71), 0),
        "block_col": draw_block_col(jax.random.fold_in(streams_of[8], 71), 0),
        "block_count": draw_block_count(jax.random.fold_in(streams_of[8], 71), 0),
        "block_samples": place_ends(jax.random.randint(streams_of[4], (N_ROWS, N_BLK, N_BLK, CAP), 1, 9), jax.random.fold_in(streams_of[4], 1), 1, 8).astype(jnp.int32),
        "row_degree": draw_row_degree(jax.random.fold_in(streams_of[8], 71), 0),
        "col_degree": jnp.clip(jnp.exp(math.log(8.0) - 2.0794415 * jax.random.uniform(streams_of[6], (N_BLK, SLAB), jnp.float32) ** level_of(streams_of[6], (N_BLK, SLAB), ((0, 4), (1, 8)), -0.2, 0.2)), 1.0, 8.0),
        "test_matrix": noise(streams_of[7], (N_BLK, SLAB, SKETCH), 1.0, 6.0, ((0, 4), (1, 8))),
    }


scale_factor = 16.0

def tile_update(running, weights, rows_idx, cols_idx, live_count, samples, row_deg, slab_rows, slab_deg):
    block_edge = weights.shape[-1]
    capacity = weights.shape[0]
    band_blocks = running.shape[0]
    slab_blocks = slab_rows.shape[0] // block_edge
    slab_tiles = slab_rows.reshape(slab_blocks, block_edge, slab_rows.shape[1])
    picked = slab_tiles[cols_idx].astype(jnp.float32)
    col_d = slab_deg.reshape(slab_blocks, block_edge)[cols_idx]
    row_d = row_deg.reshape(band_blocks, block_edge)[rows_idx]
    scaled_ratio = scale_factor * weights.astype(jnp.float32) / (samples.astype(jnp.float32)[:, None, None] * row_d[:, :, None] * col_d[:, None, :])
    entries = jnp.log(jnp.maximum(scaled_ratio, 1.0)).astype(jnp.bfloat16).astype(jnp.float32)
    products = jnp.einsum('kij,kjc->kic', entries, picked, precision=lax.Precision.HIGHEST)
    alive_mask = (jnp.arange(capacity, dtype=jnp.int32) < live_count).astype(jnp.float32)
    chooser = (rows_idx[None, :] == jnp.arange(band_blocks, dtype=jnp.int32)[:, None]).astype(jnp.float32) * alive_mask[None, :]
    return running + jnp.einsum('rk,kic->ric', chooser, products, precision=lax.Precision.HIGHEST)

def reference(block_weight, block_row, block_col, block_count, block_samples, row_degree, col_degree, test_matrix):

    def one_band(index):
        r = index // N_BLK
        b = index % N_BLK
        weights = block_weight[r, b]
        running = jnp.zeros((RB_DEV, BLK, SKETCH), jnp.float32)
        for s in range(N_BLK):
            running = tile_update(running, weights[s], block_row[r, b, s], block_col[r, b, s], block_count[r, b, s], block_samples[r, b, s], row_degree[r, b], test_matrix[s], col_degree[s])
        return running
    sketches = lax.map(one_band, jnp.arange(N_ROWS * N_BLK, dtype=jnp.int32))
    flat_rows = sketches.reshape(-1, SKETCH)
    gram_total = jnp.dot(flat_rows.T.astype(jnp.float32), flat_rows.astype(jnp.float32), precision=lax.Precision.HIGHEST, preferred_element_type=jnp.float32)
    lower_factor = jnp.linalg.cholesky(gram_total)
    root = jnp.sqrt(jnp.float32(flat_rows.shape[0]))
    basis_rows = lax.linalg.triangular_solve(lower_factor, flat_rows, left_side=False, lower=True, transpose_a=True) * root
    return (basis_rows.reshape(N_ROWS, N_BLK, BAND, SKETCH), lower_factor.T / root)
```

```python
import functools
import math

import jax
import jax.numpy as jnp
from jax import lax
from jax.experimental import pallas as pl
from jax.experimental.pallas import tpu as pltpu
from jax.sharding import PartitionSpec as P

SCALE = 16.0
GROUP = 4
CHUNK = 8


def sketch_kernel(tile, w_hbm, row_s, col_s, cnt_s, samp_s, tab_s, rd_ref, g_ref,
                  hi_ref, lo_ref, gram_ref, wbuf, x_ref, rb_ref, lc_ref, acc_ref, sem,
                  off_s, cur_s, ct_s):
    slabs, cap = w_hbm.shape[0], w_hbm.shape[1]
    bands = rd_ref.shape[0]
    n = tile
    trash = x_ref.shape[0] - 1
    zero = trash - 1
    chunks = cap // CHUNK

    def copy(s, c):
        return pltpu.make_async_copy(w_hbm.at[s, pl.ds(c * CHUNK, CHUNK)], wbuf.at[s, pl.ds(c * CHUNK, CHUNK)],
                                     sem.at[s, c])

    for s in range(slabs):
        for c in range(chunks):
            @pl.when(c * CHUNK < cnt_s[s])
            def _():
                copy(s, c).start()

    for q in range(bands):
        rb_ref[q] = jnp.transpose(jnp.broadcast_to(1.0 / rd_ref[q:q + 1, :], (n, n)))
    def deg(l, carry):
        d = g_ref[l, n:n + 16, :].astype(jnp.float32)
        lc_ref[l] = jnp.broadcast_to(jnp.log(d[0:1] + d[1:2] + d[2:3]), (8, n))
        return carry
    lax.fori_loop(0, g_ref.shape[0], deg, 0)

    for q in range(bands):
        cur_s[q] = 0
    for s in range(slabs):
        def count(k, carry):
            q = row_s[s, k]
            cur_s[q] = cur_s[q] + 1
            return carry
        lax.fori_loop(0, cnt_s[s], count, 0)
    total = jnp.int32(0)
    most = jnp.int32(0)
    for q in range(bands):
        c = cur_s[q]
        off_s[q] = total
        off_s[bands + q] = total + c
        cur_s[q] = total
        total = total + ((c + 1) // 2) * 2
        most = jnp.maximum(most, c)
    x_ref[zero] = jnp.full((n, n), -1e30, jnp.float32)
    ct_s[zero] = 0

    for s in range(slabs):
        live = cnt_s[s]
        def chunk(c, carry):
            copy(s, c).wait()
            for g0 in range(0, CHUNK, GROUP):
                todo = []
                for j in range(GROUP):
                    k = c * CHUNK + g0 + j
                    ok = k < live
                    q = row_s[s, k]
                    p = cur_s[q]
                    cur_s[q] = p + ok.astype(jnp.int32)
                    dest = jnp.where(ok, p, trash)
                    ct_s[dest] = tab_s[col_s[s, k] * slabs + s]
                    todo.append((k, q, dest, SCALE / samp_s[s, k].astype(jnp.float32)))
                out = []
                for k, q, dest, sc in todo:
                    out.append(jnp.log(wbuf[s, k].astype(jnp.float32) * (rb_ref[q] * sc)))
                for (k, q, dest, sc), o in zip(todo, out):
                    x_ref[dest] = o
            return carry
        lax.fori_loop(0, (live + CHUNK - 1) // CHUNK, chunk, 0)

    acc_ref[...] = jnp.zeros_like(acc_ref)

    def step(it, carry):
        for q in range(bands):
            e, t = [], []
            for j in range(2):
                i = off_s[q] + 2 * it + j
                i = jnp.where(i < off_s[bands + q], i, zero)
                l = ct_s[i]
                y = x_ref[i].reshape(n // 8, 8, n) - lc_ref[l][None]
                e.append(jnp.maximum(y, 0.0).reshape(n, n).astype(jnp.bfloat16))
                t.append(g_ref[l, 0:n, :])
            acc_ref[q] += jnp.dot(jnp.concatenate(e, axis=1), jnp.concatenate(t, axis=0),
                                  preferred_element_type=jnp.float32)
        return carry
    lax.fori_loop(0, (most + 1) // 2, step, 0)

    gram = jnp.zeros((n, 2 * n), jnp.float32)
    for q in range(bands):
        a = acc_ref[q]
        h = a.astype(jnp.bfloat16)
        l = (a - h.astype(jnp.float32)).astype(jnp.bfloat16)
        hi_ref[q * n:(q + 1) * n, :] = h
        lo_ref[q * n:(q + 1) * n, :] = l
        gram = gram + lax.dot_general(h, jnp.concatenate([h, l], axis=1), (((0,), (0,)), ((), ())),
                                      preferred_element_type=jnp.float32)
    cross = gram[:, n:]
    gram_ref[...] = gram[:, :n] + (cross + jnp.transpose(cross))


def sketch(w, rows, cols, counts, samples, tab, rd, g):
    slabs, cap, n, _ = w.shape
    bands = rd.shape[0]
    S = pl.BlockSpec(memory_space=pltpu.SMEM)
    V = pl.BlockSpec(memory_space=pltpu.VMEM)
    blocks = slabs * cap + 2 * bands + 2
    return pl.pallas_call(
        functools.partial(sketch_kernel, n),
        out_shape=(jax.ShapeDtypeStruct((bands * n, n), jnp.bfloat16), jax.ShapeDtypeStruct((bands * n, n), jnp.bfloat16),
                   jax.ShapeDtypeStruct((n, n), jnp.float32)),
        in_specs=[pl.BlockSpec(memory_space=pl.ANY), S, S, S, S, S, V, V],
        out_specs=(V, V, V),
        scratch_shapes=[
            pltpu.VMEM((slabs, cap, n, n), jnp.bfloat16),
            pltpu.VMEM((blocks, n, n), jnp.float32),
            pltpu.VMEM((bands, n, n), jnp.float32),
            pltpu.VMEM((g.shape[0], 8, n), jnp.float32),
            pltpu.VMEM((bands, n, n), jnp.float32),
            pltpu.SemaphoreType.DMA((slabs, cap // CHUNK)),
            pltpu.SMEM((2 * bands,), jnp.int32),
            pltpu.SMEM((bands,), jnp.int32),
            pltpu.SMEM((blocks,), jnp.int32),
        ],
        compiler_params=pltpu.CompilerParams(vmem_limit_bytes=48 << 20),
        name="sketch_gram",
    )(w, rows, cols, counts, samples, tab, rd, g)

def _rep(x, n):
    return jnp.broadcast_to(x, (1, n))

def solve_kernel(nb, root, chunk, gram_ref, hi_ref, lo_ref, basis_ref, tri_ref, m_ref, u_ref):
    n = gram_ref.shape[0]
    ii = lax.broadcasted_iota(jnp.int32, (n, n), 0)
    jj = lax.broadcasted_iota(jnp.int32, (n, n), 1)
    m_ref[:, :n] = gram_ref[...]
    m_ref[:, n:] = (ii == jj).astype(jnp.float32)
    for r0 in range(0, n, nb):
        panel = m_ref[r0:r0 + nb, :]
        left = [panel[t:t + 1, :n] for t in range(nb)]
        right = [panel[t:t + 1, n:] for t in range(nb)]
        s = [[_rep(panel[t:t + 1, r0 + u:r0 + u + 1], n) if u >= t else None for u in range(nb)] for t in range(nb)]
        for t in range(nb):
            r = lax.rsqrt(s[t][t])
            left[t] = left[t] * r
            right[t] = right[t] * r
            f = [s[t][u] * r if u > t else None for u in range(nb)]
            for u in range(t + 1, nb):
                left[u] = left[u] - f[u] * left[t]
                right[u] = right[u] - f[u] * right[t]
                for v in range(u, nb):
                    s[u][v] = s[u][v] - f[u] * f[v]
        u_l = jnp.concatenate(left, axis=0)
        u_r = jnp.concatenate(right, axis=0)
        u_ref[r0:r0 + nb, :n] = u_l
        u_ref[r0:r0 + nb, n:] = u_r
        if r0 + nb < n:
            full = jnp.concatenate([u_l, u_r], axis=1)
            upd = lax.dot_general(u_l, full, (((0,), (0,)), ((), ())), precision=lax.Precision.HIGHEST,
                                  preferred_element_type=jnp.float32)
            m_ref[r0 + nb:, :] = m_ref[r0 + nb:, :] - upd[r0 + nb:, :]
    tri_ref[...] = jnp.where(jj >= ii, u_ref[:, :n], 0.0) * (1.0 / root)
    w = jnp.where(jj <= ii, u_ref[:, n:], 0.0) * root
    wh = w.astype(jnp.bfloat16)
    wl = (w - wh.astype(jnp.float32)).astype(jnp.bfloat16)
    both = jnp.concatenate([wh, wl], axis=0)
    dims = (((1,), (1,)), ((), ()))
    for c in range(0, hi_ref.shape[0], chunk):
        h = hi_ref[c:c + chunk, :]
        l = lo_ref[c:c + chunk, :]
        a = lax.dot_general(h, both, dims, preferred_element_type=jnp.float32)
        b = lax.dot_general(l, wh, dims, preferred_element_type=jnp.float32)
        basis_ref[c:c + chunk, :] = a[:, :n] + (a[:, n:] + b)

def solve(gram, hi, lo, root, nb=16, chunk=256):
    n = gram.shape[0]
    V = pl.BlockSpec(memory_space=pltpu.VMEM)
    return pl.pallas_call(
        functools.partial(solve_kernel, nb, root, chunk),
        out_shape=(jax.ShapeDtypeStruct(hi.shape, jnp.float32), jax.ShapeDtypeStruct((n, n), jnp.float32)),
        in_specs=[V, V, V], out_specs=(V, V),
        scratch_shapes=[pltpu.VMEM((n, 2 * n), jnp.float32), pltpu.VMEM((n, 2 * n), jnp.float32)],
        compiler_params=pltpu.CompilerParams(vmem_limit_bytes=32 << 20),
        name="cholesky_basis",
    )(gram, hi, lo)


AXES = ("rows", "blk")
PAD = 16


def split3(x):
    parts = []
    for _ in range(3):
        h = lax.reduce_precision(x, 8, 7)
        parts.append(h.astype(jnp.bfloat16))
        x = x - h
    return parts


def gather_pieces(piece, n_dev):
    masks = [0]
    got = piece[None]
    bit = n_dev // 2
    while bit:
        other = lax.ppermute(got, AXES, [(i, i ^ bit) for i in range(n_dev)])
        got = jnp.concatenate([got, other], axis=0)
        masks = masks + [m ^ bit for m in masks]
        bit //= 2
    return got, masks


def sum_all(x, n_dev):
    n = x.shape[0]
    width = min(x.shape[1], x.size // n_dev)
    shares = x.reshape(n_dev, -1, width)
    mine = lax.all_to_all(shares, AXES, 0, 0, tiled=True).sum(axis=0)
    sent = jnp.broadcast_to(mine[None], shares.shape)
    return lax.all_to_all(sent, AXES, 0, 0, tiled=True).reshape(x.shape)


def body(block_weight, block_row, block_col, block_count, block_samples, row_degree, col_degree, test_matrix):
    n_rows, n_blk = lax.axis_size("rows"), lax.axis_size("blk")
    n_dev = n_rows * n_blk
    n = block_weight.shape[-1]
    piece_len, width = test_matrix.shape[1:]
    row_deg = row_degree[0, 0].reshape(-1, n)
    degs = jnp.stack(split3(col_degree[0]))
    piece = jnp.concatenate([test_matrix[0], jnp.pad(degs, ((0, PAD - 3), (0, width - piece_len)))], axis=0)
    pieces, masks = gather_pieces(piece, n_dev)
    me = lax.axis_index(AXES)
    table = me ^ jnp.asarray(masks, jnp.int32)
    if piece_len != n:
        share = n // piece_len
        ordered = pieces[jnp.argsort(table)]
        ordered = ordered.reshape(n_rows // share, share, n_blk, piece_len + PAD, width).transpose(0, 2, 1, 3, 4)
        ordered = ordered.reshape(-1, share, piece_len + PAD, width)
        tiles = ordered[:, :, :piece_len].reshape(-1, n, width)
        heads = ordered[:, :, piece_len:, :piece_len].transpose(0, 2, 1, 3).reshape(-1, PAD, n)
        pieces = jnp.concatenate([tiles, heads], axis=1)
        slots = jnp.arange(pieces.shape[0], dtype=jnp.int32)
    else:
        weights = [masks.index(1 << i) for i in range(n_dev.bit_length() - 1)]
        slots = jnp.zeros((n_dev,), jnp.int32)
        far = me ^ jnp.arange(n_dev, dtype=jnp.int32)
        for i, wt in enumerate(weights):
            slots = slots + ((far >> i) & 1) * wt
    hi, lo, gram = sketch(block_weight[0, 0], block_row[0, 0], block_col[0, 0], block_count[0, 0],
                          block_samples[0, 0], slots, row_deg, pieces)
    gram = sum_all(gram, n_dev)
    root = math.sqrt(hi.shape[0] * n_dev)
    basis, triangle = solve(gram, hi, lo, root)
    return basis[None, None], triangle


def solution(mesh):
    placed = (
        P("rows", "blk", None, None, None, None),
        P("rows", "blk", None, None),
        P("rows", "blk", None, None),
        P("rows", "blk", None),
        P("rows", "blk", None, None),
        P("rows", "blk", None),
        P("blk", "rows"),
        P("blk", "rows", None),
    )
    return jax.shard_map(
        body,
        mesh=mesh,
        in_specs=placed,
        out_specs=(P("rows", "blk", None, None), P()),
        check_vma=False,
    )
```

```python
import functools
import math

import jax
import jax.numpy as jnp
from jax import lax
from jax.experimental import pallas as pl
from jax.experimental.pallas import tpu as pltpu
from jax.sharding import PartitionSpec as P

SCALE = 16.0
MOST_SAMPLES = 8
GROUP = 16
DEPTH = 4
PAD = 16
SMEM = pl.BlockSpec(memory_space=pltpu.SMEM)
VMEM = pl.BlockSpec(memory_space=pltpu.VMEM)


def piece_kernel(test_hbm, deg_hbm, out_ref, deg_ref, sem, deg_sem):
    n = test_hbm.shape[0]
    rows = pltpu.make_async_copy(test_hbm, out_ref.at[0, pl.ds(0, n)], sem)
    degs = pltpu.make_async_copy(deg_hbm, deg_ref, deg_sem)
    rows.start()
    degs.start()
    degs.wait()
    rest = jnp.broadcast_to(deg_ref[...], (PAD, deg_ref.shape[1]))
    at = lax.broadcasted_iota(jnp.int32, rest.shape, 0)
    out = jnp.zeros_like(rest)
    for i in range(3):
        h = rest.astype(jnp.bfloat16).astype(jnp.float32)
        out = jnp.where(at == i, h, out)
        rest = rest - h
    out_ref[0, n:n + PAD, :] = out.astype(jnp.bfloat16)
    rows.wait()


def make_piece(test, deg):
    n, width = test.shape
    HBM = pl.BlockSpec(memory_space=pltpu.HBM)
    return pl.pallas_call(
        piece_kernel,
        out_shape=jax.ShapeDtypeStruct((1, n + PAD, width), jnp.bfloat16),
        in_specs=[HBM, HBM],
        out_specs=VMEM,
        scratch_shapes=[pltpu.VMEM((1, width), jnp.float32), pltpu.SemaphoreType.DMA, pltpu.SemaphoreType.DMA],
        compiler_params=pltpu.CompilerParams(vmem_limit_bytes=2 << 20),
        name="piece",
    )(pltpu.with_memory_space_constraint(test, pltpu.HBM), pltpu.with_memory_space_constraint(deg, pltpu.HBM))


def logs_kernel(slabs, first, place, *refs):
    w_hbm, rd_hbm, row_hbm, col_hbm, samp_hbm, cnt_hbm = refs[:6]
    refs = refs[7:]
    if not first:
        _, was_s, list_s = refs[:3]
        refs = refs[3:]
        x_ref, cur_s, tile_s = refs[:3]
        refs = refs[3:]
    else:
        x_ref, cur_s, tile_s, off_s = refs[:4]
        refs = refs[4:]
    wbuf, rd_ref, rb_ref, row_ref, row_s, col_s, samp_s, cnt_s, sem, small, inv_s, tab_s = refs
    n_slabs, cap = w_hbm.shape[:2]
    bands, n = rd_ref.shape
    blocks = x_ref.shape[0]
    zero, trash = blocks - 2, blocks - 1
    chunks = cap // GROUP

    def copy(s, c):
        return pltpu.make_async_copy(w_hbm.at[s, pl.ds(c * GROUP, GROUP)],
                                     wbuf.at[s - slabs[0], pl.ds(c * GROUP, GROUP)], sem.at[s - slabs[0], c])

    pairs = [(cnt_hbm, cnt_s), (rd_hbm, rd_ref), (row_hbm, row_s), (col_hbm, col_s), (samp_hbm, samp_s)]
    if first:
        pairs.append((row_hbm, row_ref))
    smalls = [pltpu.make_async_copy(p, r, small.at[i]) for i, (p, r) in enumerate(pairs)]
    for c in smalls:
        c.start()
    copy(slabs[0], 0).start()
    if first:
        x_ref[zero] = jnp.full((n, n), -1e30, jnp.float32)
    else:
        for q in range(bands):
            cur_s[q] = was_s[q]
        def keep(i, carry):
            tile_s[i] = list_s[i]
            return carry
        lax.fori_loop(0, zero, keep, 0, unroll=16)
    tile_s[zero] = 0
    for j in range(1, MOST_SAMPLES + 1):
        inv_s[j] = jnp.float32(1.0 / j)
    base, by_col, by_slab = place
    for c, v in enumerate(by_col):
        tab_s[c] = v ^ base() if base else v
    smalls[0].wait()
    for s in slabs:
        for c in range(chunks):
            if (s, c) != (slabs[0], 0):
                @pl.when(c * GROUP < cnt_s[s])
                def _():
                    copy(s, c).start()
    smalls[1].wait()
    for q in range(bands):
        rb_ref[q] = jnp.transpose(jnp.broadcast_to(SCALE / rd_ref[q:q + 1, :], (n, n)))
    for c in smalls[2:]:
        c.wait()
    if first:
        rows = row_ref[...]
        slab = lax.broadcasted_iota(jnp.int32, rows.shape, 0)
        lane = lax.broadcasted_iota(jnp.int32, rows.shape, 1)
        live = jnp.zeros(rows.shape, jnp.int32)
        for s in range(n_slabs):
            live = jnp.where(slab == s, cnt_s[s], live)
        rows = jnp.where(lane < live, rows, bands)
        off_s[0] = 0
        cur_s[0] = 0
        for q in range(1, bands + 1):
            p = jnp.sum(jnp.where(rows < q, 1.0, 0.0)).astype(jnp.int32)
            off_s[q] = p
            if q < bands:
                cur_s[q] = p

    for s in slabs:
        live = cnt_s[s]
        def chunk(c, carry):
            copy(s, c).wait()
            todo = []
            for j in range(GROUP):
                k = c * GROUP + j
                ok = k < live
                q = row_s[s, k]
                p = cur_s[q]
                cur_s[q] = p + ok.astype(jnp.int32)
                dest = jnp.where(ok, p, trash)
                tile_s[dest] = tab_s[col_s[s, k]] ^ by_slab[s]
                todo.append((k, q, dest, inv_s[samp_s[s, k]]))
            for k, q, dest, sc in todo:
                x_ref[dest] = jnp.log((wbuf[s - slabs[0], k].astype(jnp.float32) * sc) * rb_ref[q])
            return carry
        lax.fori_loop(0, (live + GROUP - 1) // GROUP, chunk, 0)


def block_logs(w, rd, rows, cols, samples, counts, held, slabs, place, state=None):
    n_slabs, cap, n, _ = w.shape
    bands = rd.shape[0]
    blocks = n_slabs * cap + 2
    first = state is None
    out = [jax.ShapeDtypeStruct((blocks, n, n), jnp.float32), jax.ShapeDtypeStruct((bands,), jnp.int32),
           jax.ShapeDtypeStruct((blocks,), jnp.int32)]
    if first:
        out.append(jax.ShapeDtypeStruct((bands + 1,), jnp.int32))
    HBM = pl.BlockSpec(memory_space=pltpu.HBM)
    ins = [pltpu.with_memory_space_constraint(v, pltpu.HBM) for v in (w, rd, rows, cols, samples, counts)]
    return pl.pallas_call(
        functools.partial(logs_kernel, slabs, first, place),
        out_shape=out,
        in_specs=[HBM] * 6 + [pl.BlockSpec(memory_space=pl.ANY)] + ([] if first else [VMEM, SMEM, SMEM]),
        out_specs=[VMEM] + [SMEM] * (len(out) - 1),
        scratch_shapes=[
            pltpu.VMEM((len(slabs), cap, n, n), jnp.bfloat16),
            pltpu.VMEM((bands, n), jnp.float32),
            pltpu.VMEM((bands, n, n), jnp.float32),
            pltpu.VMEM(rows.shape, jnp.int32),
            pltpu.SMEM(rows.shape, jnp.int32),
            pltpu.SMEM(rows.shape, jnp.int32),
            pltpu.SMEM(rows.shape, jnp.int32),
            pltpu.SMEM(counts.shape, jnp.int32),
            pltpu.SemaphoreType.DMA((len(slabs), cap // GROUP)),
            pltpu.SemaphoreType.DMA((6,)),
            pltpu.SMEM((MOST_SAMPLES + 1,), jnp.float32),
            pltpu.SMEM((len(place[1]),), jnp.int32),
        ],
        input_output_aliases={} if first else {7: 0},
        compiler_params=pltpu.CompilerParams(vmem_limit_bytes=10 << 20),
        cost_estimate=pl.CostEstimate(flops=0, bytes_accessed=len(slabs) * cap * n * n * 4, transcendentals=0),
        name="block_logs",
    )(*ins, held, *(state[:3] if state else ()))


def products_kernel(x_ref, off_s, tile_s, *refs):
    hi_ref, lo_ref, gram_ref, g_ref, lc_ref, acc_ref = refs[-6:]
    n = x_ref.shape[-1]
    bands = off_s.shape[0] - 1
    zero = x_ref.shape[0] - 2
    most = off_s[1] - off_s[0]
    for q in range(1, bands):
        most = jnp.maximum(most, off_s[q + 1] - off_s[q])

    at = 0
    for part in refs[:-6]:
        for i in range(part.shape[0]):
            g_ref[at] = part[i, 0:n, :]
            d = part[i, n:n + PAD, :].astype(jnp.float32)
            lc_ref[at] = jnp.broadcast_to(jnp.log(d[0:1] + d[1:2] + d[2:3]), (8, n))
            at += 1
    acc_ref[...] = jnp.zeros_like(acc_ref)

    def step(it, carry):
        for q in range(bands):
            e, t = [], []
            for j in range(DEPTH):
                i = off_s[q] + (it * DEPTH + j)
                i = jnp.where(i < off_s[q + 1], i, zero)
                l = tile_s[i]
                y = x_ref[i].reshape(n // 8, 8, n) - lc_ref[l][None]
                e.append(jnp.maximum(y, 0.0).reshape(n, n).astype(jnp.bfloat16))
                t.append(g_ref[l])
            acc_ref[q] += jnp.dot(jnp.concatenate(e, axis=1), jnp.concatenate(t, axis=0),
                                  preferred_element_type=jnp.float32)
        return carry
    lax.fori_loop(0, (most + DEPTH - 1) // DEPTH, step, 0)

    gram = jnp.zeros((n, 2 * n), jnp.float32)
    for q in range(bands):
        a = acc_ref[q]
        h = a.astype(jnp.bfloat16)
        l = (a - h.astype(jnp.float32)).astype(jnp.bfloat16)
        hi_ref[q * n:(q + 1) * n, :] = h
        lo_ref[q * n:(q + 1) * n, :] = l
        gram = gram + lax.dot_general(h, jnp.concatenate([h, l], axis=1), (((0,), (0,)), ((), ())),
                                      preferred_element_type=jnp.float32)
    cross = gram[:, n:]
    gram_ref[...] = gram[:, :n] + (cross + jnp.transpose(cross))


def products(x, off, tiles, parts):
    n = x.shape[-1]
    bands = off.shape[0] - 1
    total = sum(p.shape[0] for p in parts)
    return pl.pallas_call(
        products_kernel,
        out_shape=(jax.ShapeDtypeStruct((bands * n, n), jnp.bfloat16), jax.ShapeDtypeStruct((bands * n, n), jnp.bfloat16),
                   jax.ShapeDtypeStruct((n, n), jnp.float32)),
        in_specs=[VMEM, SMEM, SMEM] + [VMEM] * len(parts),
        out_specs=(VMEM, VMEM, VMEM),
        scratch_shapes=[
            pltpu.VMEM((total, n, n), jnp.bfloat16),
            pltpu.VMEM((total, 8, n), jnp.float32),
            pltpu.VMEM((bands, n, n), jnp.float32),
        ],
        compiler_params=pltpu.CompilerParams(vmem_limit_bytes=8 << 20),
        name="products_gram",
    )(x, off, tiles, *parts)


def _rep(x, n):
    return jnp.broadcast_to(x, (1, n))

def split(x):
    h = x.astype(jnp.bfloat16)
    x = x - h.astype(jnp.float32)
    m = x.astype(jnp.bfloat16)
    return h, m, (x - m.astype(jnp.float32)).astype(jnp.bfloat16)


def stacked_gram(a, b):
    ah, am, al = split(a)
    bh, bm, bl = split(b)
    return lax.dot_general(jnp.concatenate([ah, ah, am, am, ah, al], axis=0),
                           jnp.concatenate([bh, bm, bh, bm, bl, bh], axis=0),
                           (((0,), (0,)), ((), ())), preferred_element_type=jnp.float32)


def solve_kernel(nb, root, chunk, gram_ref, hi_ref, lo_ref, basis_ref, tri_ref, m_ref, u_ref):
    n = gram_ref.shape[0]
    ii = lax.broadcasted_iota(jnp.int32, (n, n), 0)
    jj = lax.broadcasted_iota(jnp.int32, (n, n), 1)
    m_ref[:, :n] = gram_ref[...]
    m_ref[:, n:] = (ii == jj).astype(jnp.float32)
    for r0 in range(0, n, nb):
        panel = m_ref[r0:r0 + nb, :]
        left = [panel[t:t + 1, :n] for t in range(nb)]
        right = [panel[t:t + 1, n:] for t in range(nb)]
        s = [[_rep(panel[t:t + 1, r0 + u:r0 + u + 1], n) if u >= t else None for u in range(nb)] for t in range(nb)]
        for t in range(nb):
            r = lax.rsqrt(s[t][t])
            left[t] = left[t] * r
            right[t] = right[t] * r
            f = [s[t][u] * r if u > t else None for u in range(nb)]
            for u in range(t + 1, nb):
                left[u] = left[u] - f[u] * left[t]
                right[u] = right[u] - f[u] * right[t]
                for v in range(u, nb):
                    s[u][v] = s[u][v] - f[u] * f[v]
        u_l = jnp.concatenate(left, axis=0)
        u_r = jnp.concatenate(right, axis=0)
        u_ref[r0:r0 + nb, :n] = u_l
        u_ref[r0:r0 + nb, n:] = u_r
        if r0 + nb < n:
            upd = stacked_gram(u_l, jnp.concatenate([u_l, u_r], axis=1))
            m_ref[r0 + nb:, :] = m_ref[r0 + nb:, :] - upd[r0 + nb:, :]
    tri_ref[...] = jnp.where(jj >= ii, u_ref[:, :n], 0.0) * (1.0 / root)
    w = jnp.where(jj <= ii, u_ref[:, n:], 0.0) * root
    wh = w.astype(jnp.bfloat16)
    wl = (w - wh.astype(jnp.float32)).astype(jnp.bfloat16)
    both = jnp.concatenate([wh, wl], axis=0)
    dims = (((1,), (1,)), ((), ()))
    for c in range(0, hi_ref.shape[0], chunk):
        h = hi_ref[c:c + chunk, :]
        l = lo_ref[c:c + chunk, :]
        a = lax.dot_general(h, both, dims, preferred_element_type=jnp.float32)
        b = lax.dot_general(l, wh, dims, preferred_element_type=jnp.float32)
        basis_ref[c:c + chunk, :] = a[:, :n] + (a[:, n:] + b)

def solve(gram, hi, lo, root, nb=16, chunk=256):
    n = gram.shape[0]
    V = pl.BlockSpec(memory_space=pltpu.VMEM)
    return pl.pallas_call(
        functools.partial(solve_kernel, nb, root, chunk),
        out_shape=(jax.ShapeDtypeStruct(hi.shape, jnp.float32), jax.ShapeDtypeStruct((n, n), jnp.float32)),
        in_specs=[V, V, V], out_specs=(V, V),
        scratch_shapes=[pltpu.VMEM((n, 2 * n), jnp.float32), pltpu.VMEM((n, 2 * n), jnp.float32)],
        compiler_params=pltpu.CompilerParams(vmem_limit_bytes=6 << 20),
        name="cholesky_basis",
    )(gram, hi, lo)


AXES = ("rows", "blk")


def send(x, mask, n_dev):
    return lax.ppermute(x, AXES, [(i, i ^ mask) for i in range(n_dev)])


def sum_all(x, n_dev):
    width = min(x.shape[1], x.size // n_dev)
    shares = x.reshape(n_dev, -1, width)
    mine = lax.all_to_all(shares, AXES, 0, 0, tiled=True).sum(axis=0)
    sent = jnp.broadcast_to(mine[None], shares.shape)
    return lax.all_to_all(sent, AXES, 0, 0, tiled=True).reshape(x.shape)


def body(block_weight, block_row, block_col, block_count, block_samples, row_degree, col_degree, test_matrix):
    n_rows, n_blk = lax.axis_size("rows"), lax.axis_size("blk")
    n_dev = n_rows * n_blk
    weights = block_weight[0, 0]
    n_slabs, _, n, _ = weights.shape
    piece_len, width = test_matrix.shape[1:]
    row_deg = row_degree[0, 0].reshape(-1, n)
    me = lax.axis_index(AXES)

    if piece_len == n:
        piece = make_piece(test_matrix[0], col_degree)
    else:
        degs = jnp.broadcast_to(jnp.pad(col_degree, ((0, 0), (0, width - piece_len)), constant_values=1.0), (PAD, width))
        rows_at = lax.broadcasted_iota(jnp.int32, degs.shape, 0)
        head = jnp.zeros_like(degs)
        for i in range(3):
            h = lax.reduce_precision(degs, 8, 7)
            head = jnp.where(rows_at == i, h, head)
            degs = degs - h
        piece = jnp.concatenate([test_matrix[0], head.astype(jnp.bfloat16)], axis=0)[None]

    bits = [1 << i for i in range(1, n_dev.bit_length() - 1)]
    plane, line = bits[:2], bits[2:][::-1]
    masks = [0, plane[0], plane[1], plane[0] ^ plane[1]]
    group = jnp.concatenate([piece] + [send(piece, m, n_dev) for m in masks[1:]], axis=0)
    parts = [group]
    half = n_slabs // 2
    slab_sets = [range(half), range(half, n_slabs)]
    order = list(masks)
    for m in line:
        order = order + [v ^ m for v in order]
    order = order + [v ^ 1 for v in order]
    n_cols = n_rows * piece_len // n
    if piece_len == n:
        weights_of = [order.index(1 << i) for i in range(n_dev.bit_length() - 1)]
        spread = lambda v: sum(w for i, w in enumerate(weights_of) if v >> i & 1)
        def base():
            at = lax.axis_index("rows") * n_blk + lax.axis_index("blk")
            return sum(((at >> i) & 1) * w for i, w in enumerate(weights_of))
        place = (base, [spread(c * n_blk) for c in range(n_cols)], [spread(s) for s in range(n_blk)])
    else:
        place = (None, [c * n_blk for c in range(n_cols)], list(range(n_blk)))
    tables = (row_deg, block_row[0, 0], block_col[0, 0], block_samples[0, 0], block_count[0, 0])
    state = None
    swapped = []
    for step, m in enumerate(line):
        got = send(group, m, n_dev)
        swapped.append(send(parts[-1], 1, n_dev))
        if step >= len(line) - 2:
            slabs = slab_sets[step - (len(line) - 2)]
            state = [*block_logs(weights, *tables, group, slabs, place, state), *(state or [])[3:]]
            got, *state = lax.optimization_barrier((got, *state))
        parts.append(got)
        group = jnp.concatenate([group, got], axis=0)
    swapped.append(send(parts[-1], 1, n_dev))
    parts = parts + swapped
    if piece_len != n:
        share = n // piece_len
        pieces = jnp.concatenate(parts, axis=0)[jnp.argsort(me ^ jnp.asarray(order, jnp.int32))]
        pieces = pieces.reshape(n_rows // share, share, n_blk, piece_len + PAD, width).transpose(0, 2, 1, 3, 4)
        pieces = pieces.reshape(-1, share, piece_len + PAD, width)
        tiles = pieces[:, :, :piece_len].reshape(-1, n, width)
        heads = pieces[:, :, piece_len:, :piece_len].transpose(0, 2, 1, 3).reshape(-1, PAD, n)
        parts = [jnp.concatenate([tiles, heads], axis=1)]
    hi, lo, gram = products(state[0], state[3], state[2], parts)
    gram = sum_all(gram, n_dev)
    basis, triangle = solve(gram, hi, lo, math.sqrt(hi.shape[0] * n_dev))
    return basis[None, None], triangle


def solution(mesh):
    placed = (
        P("rows", "blk", None, None, None, None),
        P("rows", "blk", None, None),
        P("rows", "blk", None, None),
        P("rows", "blk", None),
        P("rows", "blk", None, None),
        P("rows", "blk", None),
        P("blk", "rows"),
        P("blk", "rows", None),
    )
    return jax.shard_map(
        body,
        mesh=mesh,
        in_specs=placed,
        out_specs=(P("rows", "blk", None, None), P()),
        check_vma=False,
    )
```

```python
import functools
import math

import jax
import jax.numpy as jnp
from jax import lax
from jax.experimental import pallas as pl
from jax.experimental.pallas import tpu as pltpu
from jax.sharding import PartitionSpec as P

SCALE = 16.0
MOST_SAMPLES = 8
GROUP = 16
DEPTH = 4
ITEMS = (32, 16)
PLACES = 1 << 16
PAD = 16
SMEM = pl.BlockSpec(memory_space=pltpu.SMEM)
VMEM = pl.BlockSpec(memory_space=pltpu.VMEM)


def piece_kernel(test_hbm, deg_hbm, out_ref, deg_ref, sem, deg_sem):
    n = test_hbm.shape[0]
    rows = pltpu.make_async_copy(test_hbm, out_ref.at[0, pl.ds(0, n)], sem)
    degs = pltpu.make_async_copy(deg_hbm, deg_ref, deg_sem)
    rows.start()
    degs.start()
    degs.wait()
    rest = jnp.broadcast_to(deg_ref[...], (PAD, deg_ref.shape[1]))
    at = lax.broadcasted_iota(jnp.int32, rest.shape, 0)
    out = jnp.zeros_like(rest)
    for i in range(3):
        h = rest.astype(jnp.bfloat16).astype(jnp.float32)
        out = jnp.where(at == i, h, out)
        rest = rest - h
    out_ref[0, n:n + PAD, :] = out.astype(jnp.bfloat16)
    rows.wait()


def make_piece(test, deg):
    n, width = test.shape
    HBM = pl.BlockSpec(memory_space=pltpu.HBM)
    return pl.pallas_call(
        piece_kernel,
        out_shape=jax.ShapeDtypeStruct((1, n + PAD, width), jnp.bfloat16),
        in_specs=[HBM, HBM],
        out_specs=VMEM,
        scratch_shapes=[pltpu.VMEM((1, width), jnp.float32), pltpu.SemaphoreType.DMA, pltpu.SemaphoreType.DMA],
        compiler_params=pltpu.CompilerParams(vmem_limit_bytes=2 << 20),
        name="piece",
    )(pltpu.with_memory_space_constraint(test, pltpu.HBM), pltpu.with_memory_space_constraint(deg, pltpu.HBM))


def logs_kernel(slabs, first, place, *refs):
    w_hbm, rd_hbm, row_hbm, col_hbm, samp_hbm, cnt_hbm = refs[:6]
    refs = refs[7:]
    if not first:
        _, was_s, list_s, rb_ref = refs[:4]
        refs = refs[4:]
        x_ref, cur_s, tile_s = refs[:3]
        refs = refs[3:]
    else:
        x_ref, cur_s, tile_s, rb_ref, off_s, item_s = refs[:6]
        refs = refs[6:]
    wbuf, rd_ref, row_ref, row_s, col_s, samp_s, cnt_s, sem, small, inv_s, tab_s = refs
    n_slabs, cap = w_hbm.shape[:2]
    bands, n = rb_ref.shape[:2]
    blocks = x_ref.shape[0]
    zero, trash = blocks - 2, blocks - 1
    chunks = cap // GROUP

    def copy(s, c):
        return pltpu.make_async_copy(w_hbm.at[s, pl.ds(c * GROUP, GROUP)],
                                     wbuf.at[s - slabs[0], pl.ds(c * GROUP, GROUP)], sem.at[s - slabs[0], c])

    pairs = [(cnt_hbm, cnt_s), (row_hbm, row_s), (col_hbm, col_s), (samp_hbm, samp_s)]
    if first:
        pairs += [(rd_hbm, rd_ref), (row_hbm, row_ref)]
    smalls = [pltpu.make_async_copy(p, r, small.at[i]) for i, (p, r) in enumerate(pairs)]
    for c in smalls:
        c.start()
    copy(slabs[0], 0).start()
    if first:
        x_ref[zero] = jnp.full((n, n), -1e30, jnp.float32)
    else:
        for q in range(bands):
            cur_s[q] = was_s[q]
        def keep(i, carry):
            tile_s[i] = list_s[i]
            return carry
        lax.fori_loop(0, zero, keep, 0, unroll=16)
    tile_s[zero] = 0
    for j in range(1, MOST_SAMPLES + 1):
        inv_s[j] = jnp.float32(1.0 / j)
    base, by_col, by_slab = place
    for c, v in enumerate(by_col):
        tab_s[c] = v ^ base() if base else v
    smalls[0].wait()
    for s in slabs:
        for c in range(chunks):
            if (s, c) != (slabs[0], 0):
                @pl.when(c * GROUP < cnt_s[s])
                def _():
                    copy(s, c).start()
    for c in smalls[1:]:
        c.wait()
    if first:
        for q in range(bands):
            rb_ref[q] = jnp.transpose(jnp.broadcast_to(SCALE / rd_ref[q:q + 1, :], (n, n)))
        rows = row_ref[...]
        slab = lax.broadcasted_iota(jnp.int32, rows.shape, 0)
        lane = lax.broadcasted_iota(jnp.int32, rows.shape, 1)
        live = jnp.zeros(rows.shape, jnp.int32)
        for s in range(n_slabs):
            live = jnp.where(slab == s, cnt_s[s], live)
        rows = jnp.where(lane < live, rows, bands)
        off_s[0] = 0
        cur_s[0] = 0
        for q in range(1, bands + 1):
            p = jnp.sum(jnp.where(rows < q, 1.0, 0.0)).astype(jnp.int32)
            off_s[q] = p
            if q < bands:
                cur_s[q] = p
        rounds = item_s.shape[0] // bands - 2
        starts = [off_s[q] for q in range(bands + 1)]
        count = jnp.int32(0)
        for it in range(rounds):
            for q in range(bands):
                first_at = starts[q] + it * DEPTH
                item_s[count] = q * PLACES + first_at
                count = count + (first_at < starts[q + 1]).astype(jnp.int32)
        for i in range(ITEMS[0]):
            item_s[count + i] = PLACES - 1 - DEPTH
        off_s[bands + 1] = count

    for s in slabs:
        live = cnt_s[s]
        def chunk(c, carry):
            copy(s, c).wait()
            todo = []
            for j in range(GROUP):
                k = c * GROUP + j
                ok = k < live
                q = row_s[s, k]
                p = cur_s[q]
                cur_s[q] = p + ok.astype(jnp.int32)
                dest = jnp.where(ok, p, trash)
                tile_s[dest] = tab_s[col_s[s, k]] ^ by_slab[s]
                todo.append((k, q, dest, inv_s[samp_s[s, k]]))
            for k, q, dest, sc in todo:
                x_ref[dest] = jnp.log((wbuf[s - slabs[0], k].astype(jnp.float32) * sc) * rb_ref[q])
            return carry
        lax.fori_loop(0, (live + GROUP - 1) // GROUP, chunk, 0)


def block_logs(w, rd, rows, cols, samples, counts, held, slabs, place, state=None):
    n_slabs, cap, n, _ = w.shape
    bands = rd.shape[0]
    blocks = n_slabs * cap + 2
    first = state is None
    out = [jax.ShapeDtypeStruct((blocks, n, n), jnp.float32), jax.ShapeDtypeStruct((bands,), jnp.int32),
           jax.ShapeDtypeStruct((blocks,), jnp.int32)]
    if first:
        rounds = -(-n_slabs * len(place[1]) // DEPTH)
        out += [jax.ShapeDtypeStruct((bands, n, n), jnp.float32), jax.ShapeDtypeStruct((bands + 2,), jnp.int32),
                jax.ShapeDtypeStruct(((rounds + 2) * bands,), jnp.int32)]
    HBM = pl.BlockSpec(memory_space=pltpu.HBM)
    ins = [pltpu.with_memory_space_constraint(v, pltpu.HBM) for v in (w, rd, rows, cols, samples, counts)]
    return pl.pallas_call(
        functools.partial(logs_kernel, slabs, first, place),
        out_shape=out,
        in_specs=[HBM] * 6 + [pl.BlockSpec(memory_space=pl.ANY)] + ([] if first else [VMEM, SMEM, SMEM, VMEM]),
        out_specs=[VMEM, SMEM, SMEM] + ([VMEM, SMEM, SMEM] if first else []),
        scratch_shapes=[
            pltpu.VMEM((len(slabs), cap, n, n), jnp.bfloat16),
            pltpu.VMEM((bands, n), jnp.float32),
            pltpu.VMEM(rows.shape, jnp.int32),
            pltpu.SMEM(rows.shape, jnp.int32),
            pltpu.SMEM(rows.shape, jnp.int32),
            pltpu.SMEM(rows.shape, jnp.int32),
            pltpu.SMEM(counts.shape, jnp.int32),
            pltpu.SemaphoreType.DMA((len(slabs), cap // GROUP)),
            pltpu.SemaphoreType.DMA((6,)),
            pltpu.SMEM((MOST_SAMPLES + 1,), jnp.float32),
            pltpu.SMEM((len(place[1]),), jnp.int32),
        ],
        input_output_aliases={} if first else {7: 0},
        compiler_params=pltpu.CompilerParams(vmem_limit_bytes=12 << 20),
        cost_estimate=pl.CostEstimate(flops=0, bytes_accessed=len(slabs) * cap * n * n * 4, transcendentals=0),
        name="block_logs",
    )(*ins, held, *(state[:4] if state else ()))


def products_kernel(x_ref, off_s, item_s, tile_s, *refs):
    hi_ref, lo_ref, gram_ref, g_ref, lc_ref, acc_ref = refs[-6:]
    n = x_ref.shape[-1]
    bands = off_s.shape[0] - 2
    zero = x_ref.shape[0] - 2

    at = 0
    for part in refs[:-6]:
        for i in range(part.shape[0]):
            g_ref[at] = part[i, 0:n, :]
            d = part[i, n:n + PAD, :].astype(jnp.float32)
            lc_ref[at] = jnp.broadcast_to(jnp.log(d[0:1] + d[1:2] + d[2:3]), (8, n))
            at += 1
    acc_ref[...] = jnp.zeros_like(acc_ref)

    def step(first, items):
        def run(it, carry):
            for k in range(items):
                word = item_s[first + it * items + k]
                q = word >> 16
                last = off_s[q + 1]
                e, t = [], []
                for j in range(DEPTH):
                    i = (word & (PLACES - 1)) + j
                    i = jnp.where(i < last, i, zero)
                    l = tile_s[i]
                    y = x_ref[i].reshape(n // 8, 8, n) - lc_ref[l][None]
                    e.append(jnp.maximum(y, 0.0).reshape(n, n).astype(jnp.bfloat16))
                    t.append(g_ref[l])
                acc_ref[q] += jnp.dot(jnp.concatenate(e, axis=1), jnp.concatenate(t, axis=0),
                                      preferred_element_type=jnp.float32)
            return carry
        return run
    long, short = ITEMS
    count = off_s[bands + 1]
    longs = (count + long - short - 1) // long
    lax.fori_loop(0, longs, step(0, long), 0)
    lax.fori_loop(0, (jnp.maximum(count - longs * long, 0) + short - 1) // short, step(longs * long, short), 0)

    gram = jnp.zeros((n, 2 * n), jnp.float32)
    for q in range(bands):
        a = acc_ref[q]
        h = a.astype(jnp.bfloat16)
        l = (a - h.astype(jnp.float32)).astype(jnp.bfloat16)
        hi_ref[q * n:(q + 1) * n, :] = h
        lo_ref[q * n:(q + 1) * n, :] = l
        gram = gram + lax.dot_general(h, jnp.concatenate([h, l], axis=1), (((0,), (0,)), ((), ())),
                                      preferred_element_type=jnp.float32)
    cross = gram[:, n:]
    gram_ref[...] = gram[:, :n] + (cross + jnp.transpose(cross))


def products(x, off, items, tiles, parts):
    n = x.shape[-1]
    bands = off.shape[0] - 2
    total = sum(p.shape[0] for p in parts)
    return pl.pallas_call(
        products_kernel,
        out_shape=(jax.ShapeDtypeStruct((bands * n, n), jnp.bfloat16), jax.ShapeDtypeStruct((bands * n, n), jnp.bfloat16),
                   jax.ShapeDtypeStruct((n, n), jnp.float32)),
        in_specs=[VMEM, SMEM, SMEM, SMEM] + [VMEM] * len(parts),
        out_specs=(VMEM, VMEM, VMEM),
        scratch_shapes=[
            pltpu.VMEM((total, n, n), jnp.bfloat16),
            pltpu.VMEM((total, 8, n), jnp.float32),
            pltpu.VMEM((bands, n, n), jnp.float32),
        ],
        compiler_params=pltpu.CompilerParams(vmem_limit_bytes=8 << 20),
        name="products_gram",
    )(x, off, items, tiles, *parts)


def _rep(x, n):
    return jnp.broadcast_to(x, (1, n))

def split(x):
    h = x.astype(jnp.bfloat16)
    x = x - h.astype(jnp.float32)
    m = x.astype(jnp.bfloat16)
    return h, m, (x - m.astype(jnp.float32)).astype(jnp.bfloat16)


def stacked_gram(x):
    h, m, l = split(x)
    return lax.dot_general(jnp.concatenate([h, h, m, m, h, l], axis=0), jnp.concatenate([h, m, h, m, l, h], axis=0),
                           (((0,), (0,)), ((), ())), preferred_element_type=jnp.float32)


def solve_kernel(nb, root, chunk, gram_ref, hi_ref, lo_ref, basis_ref, tri_ref, m_ref):
    n = gram_ref.shape[0]
    lane = lax.broadcasted_iota(jnp.int32, (1, n), 1)
    m_ref[...] = gram_ref[...]
    for r0 in range(0, n, nb):
        panel = m_ref[r0:r0 + nb, :]
        s = [[_rep(panel[t:t + 1, r0 + u:r0 + u + 1], n) if u >= t else None for u in range(nb)] for t in range(nb)]
        inside = (lane >= r0) & (lane < r0 + nb)
        rows = [jnp.where(inside, jnp.where(lane == r0 + t, 1.0, 0.0), panel[t:t + 1, :]) for t in range(nb)]
        tops = []
        for t in range(nb):
            r = lax.rsqrt(s[t][t])
            rows[t] = rows[t] * r
            f = [s[t][u] * r if u >= t else None for u in range(nb)]
            for u in range(t + 1, nb):
                rows[u] = rows[u] - f[u] * rows[t]
                for v in range(u, nb):
                    s[u][v] = s[u][v] - f[u] * f[v]
            top = rows[t]
            for u in range(t, nb):
                top = jnp.where(lane == r0 + u, f[u], top)
            tops.append(top)
        x = jnp.concatenate(rows, axis=0)
        tri_ref[r0:r0 + nb, :] = jnp.concatenate(tops, axis=0)
        m_ref[r0:r0 + nb, :] = x
        if r0 + nb < n:
            below = m_ref[r0 + nb:, :]
            m_ref[r0 + nb:, :] = jnp.where(inside, 0.0, below) - stacked_gram(x)[r0 + nb:, :]
    ii = lax.broadcasted_iota(jnp.int32, (n, n), 0)
    jj = lax.broadcasted_iota(jnp.int32, (n, n), 1)
    tri_ref[...] = jnp.where(jj >= ii, tri_ref[...], 0.0) * (1.0 / root)
    w = jnp.where(jj <= ii, m_ref[...], 0.0) * root
    wh = w.astype(jnp.bfloat16)
    wl = (w - wh.astype(jnp.float32)).astype(jnp.bfloat16)
    both = jnp.concatenate([wh, wl], axis=0)
    dims = (((1,), (1,)), ((), ()))
    for c in range(0, hi_ref.shape[0], chunk):
        h = hi_ref[c:c + chunk, :]
        l = lo_ref[c:c + chunk, :]
        a = lax.dot_general(h, both, dims, preferred_element_type=jnp.float32)
        b = lax.dot_general(l, wh, dims, preferred_element_type=jnp.float32)
        basis_ref[c:c + chunk, :] = a[:, :n] + (a[:, n:] + b)


def solve(gram, hi, lo, root, nb=16, chunk=512):
    n = gram.shape[0]
    V = pl.BlockSpec(memory_space=pltpu.VMEM)
    return pl.pallas_call(
        functools.partial(solve_kernel, nb, root, chunk),
        out_shape=(jax.ShapeDtypeStruct(hi.shape, jnp.float32), jax.ShapeDtypeStruct((n, n), jnp.float32)),
        in_specs=[V, V, V], out_specs=(V, V),
        scratch_shapes=[pltpu.VMEM((n, n), jnp.float32)],
        compiler_params=pltpu.CompilerParams(vmem_limit_bytes=6 << 20),
        name="cholesky_basis",
    )(gram, hi, lo)


AXES = ("rows", "blk")
STAGES = ((0, 1), (1, 2), (0, 0), (2, 4))


def send(x, mask, n_dev):
    return lax.ppermute(x, AXES, [(i, i ^ mask) for i in range(n_dev)])


def sum_all(x, n_dev):
    width = min(x.shape[1], x.size // n_dev)
    shares = x.reshape(n_dev, -1, width)
    mine = lax.all_to_all(shares, AXES, 0, 0, tiled=True).sum(axis=0)
    sent = jnp.broadcast_to(mine[None], shares.shape)
    return lax.all_to_all(sent, AXES, 0, 0, tiled=True).reshape(x.shape)


def body(block_weight, block_row, block_col, block_count, block_samples, row_degree, col_degree, test_matrix):
    n_rows, n_blk = lax.axis_size("rows"), lax.axis_size("blk")
    n_dev = n_rows * n_blk
    weights = block_weight[0, 0]
    n_slabs, _, n, _ = weights.shape
    piece_len, width = test_matrix.shape[1:]
    row_deg = row_degree[0, 0].reshape(-1, n)
    me = lax.axis_index(AXES)

    if piece_len == n:
        piece = make_piece(test_matrix[0], col_degree)
    else:
        degs = jnp.broadcast_to(jnp.pad(col_degree, ((0, 0), (0, width - piece_len)), constant_values=1.0), (PAD, width))
        rows_at = lax.broadcasted_iota(jnp.int32, degs.shape, 0)
        head = jnp.zeros_like(degs)
        for i in range(3):
            h = lax.reduce_precision(degs, 8, 7)
            head = jnp.where(rows_at == i, h, head)
            degs = degs - h
        piece = jnp.concatenate([test_matrix[0], head.astype(jnp.bfloat16)], axis=0)[None]

    bits = [1 << i for i in range(1, n_dev.bit_length() - 1)]
    line, plane = bits[2:][::-1], (bits[0], bits[1], bits[0] ^ bits[1])
    order = [0]
    for m in line:
        order = order + [v ^ m for v in order]
    order = [v ^ m for m in (0, *plane) for v in order]
    order = order + [v ^ 1 for v in order]
    n_cols = n_rows * piece_len // n
    if piece_len == n:
        weights_of = [order.index(1 << i) for i in range(n_dev.bit_length() - 1)]
        spread = lambda v: sum(w for i, w in enumerate(weights_of) if v >> i & 1)
        def base():
            at = lax.axis_index("rows") * n_blk + lax.axis_index("blk")
            return sum(((at >> i) & 1) * w for i, w in enumerate(weights_of))
        place = (base, [spread(c * n_blk) for c in range(n_cols)], [spread(s) for s in range(n_blk)])
    else:
        place = (None, [c * n_blk for c in range(n_cols)], list(range(n_blk)))
    tables = (row_deg, block_row[0, 0], block_col[0, 0], block_samples[0, 0], block_count[0, 0])
    slab_sets = [range(n_slabs * a // 4, n_slabs * b // 4) for a, b in STAGES]

    def logs(state, held, stage):
        if not len(slab_sets[stage]):
            return state
        return [*block_logs(weights, *tables, held, slab_sets[stage], place, state), *(state or [])[3:]]

    group, state = piece, None
    for step, m in enumerate(line):
        got = send(group, m, n_dev)
        stage = step - (len(line) - 2)
        if stage >= 0:
            state = logs(state, group, stage)
            if state:
                got, *state = lax.optimization_barrier((got, *state))
        group = jnp.concatenate([group, got], axis=0)
    one, two = plane[:2]
    near = send(group, two, n_dev)
    side = send(group, one, n_dev)
    swapped = send(group, 1, n_dev)
    state = logs(state, group, 2)
    near, *state = lax.optimization_barrier((near, *state))
    far = send(near, one, n_dev)
    near_swapped = send(near, 1, n_dev)
    state = logs(state, near, 3)
    side, far, swapped, near_swapped, state[0] = lax.optimization_barrier((side, far, swapped, near_swapped, state[0]))
    parts = [group, side, near, far]
    swapped = [swapped, send(side, 1, n_dev), near_swapped, send(far, 1, n_dev)]
    parts = parts + swapped
    if piece_len != n:
        share = n // piece_len
        pieces = jnp.concatenate(parts, axis=0)[jnp.argsort(me ^ jnp.asarray(order, jnp.int32))]
        pieces = pieces.reshape(n_rows // share, share, n_blk, piece_len + PAD, width).transpose(0, 2, 1, 3, 4)
        pieces = pieces.reshape(-1, share, piece_len + PAD, width)
        tiles = pieces[:, :, :piece_len].reshape(-1, n, width)
        heads = pieces[:, :, piece_len:, :piece_len].transpose(0, 2, 1, 3).reshape(-1, PAD, n)
        parts = [jnp.concatenate([tiles, heads], axis=1)]
    hi, lo, gram = products(state[0], state[4], state[5], state[2], parts)
    gram = sum_all(gram, n_dev)
    basis, triangle = solve(gram, hi, lo, math.sqrt(hi.shape[0] * n_dev))
    return basis[None, None], triangle


def solution(mesh):
    placed = (
        P("rows", "blk", None, None, None, None),
        P("rows", "blk", None, None),
        P("rows", "blk", None, None),
        P("rows", "blk", None),
        P("rows", "blk", None, None),
        P("rows", "blk", None),
        P("blk", "rows"),
        P("blk", "rows", None),
    )
    return jax.shard_map(
        body,
        mesh=mesh,
        in_specs=placed,
        out_specs=(P("rows", "blk", None, None), P()),
        check_vma=False,
    )
```

```python
import functools
import math

import jax
import jax.numpy as jnp
from jax import lax
from jax.experimental import pallas as pl
from jax.experimental.pallas import tpu as pltpu
from jax.sharding import PartitionSpec as P

SCALE = 16.0
MOST_SAMPLES = 8
GROUP = 16
DEPTH = 4
ITEMS = (32, 16)
PLACES = 1 << 16
PAD = 16
SMEM = pl.BlockSpec(memory_space=pltpu.SMEM)
VMEM = pl.BlockSpec(memory_space=pltpu.VMEM)


def piece_kernel(test_hbm, deg_hbm, out_ref, deg_ref, sem, deg_sem):
    n = test_hbm.shape[0]
    rows = pltpu.make_async_copy(test_hbm, out_ref.at[0, pl.ds(0, n)], sem)
    degs = pltpu.make_async_copy(deg_hbm, deg_ref, deg_sem)
    rows.start()
    degs.start()
    degs.wait()
    rest = jnp.broadcast_to(deg_ref[...], (PAD, deg_ref.shape[1]))
    at = lax.broadcasted_iota(jnp.int32, rest.shape, 0)
    out = jnp.zeros_like(rest)
    for i in range(3):
        h = rest.astype(jnp.bfloat16).astype(jnp.float32)
        out = jnp.where(at == i, h, out)
        rest = rest - h
    out_ref[0, n:n + PAD, :] = out.astype(jnp.bfloat16)
    rows.wait()


def make_piece(test, deg):
    n, width = test.shape
    HBM = pl.BlockSpec(memory_space=pltpu.HBM)
    return pl.pallas_call(
        piece_kernel,
        out_shape=jax.ShapeDtypeStruct((1, n + PAD, width), jnp.bfloat16),
        in_specs=[HBM, HBM],
        out_specs=VMEM,
        scratch_shapes=[pltpu.VMEM((1, width), jnp.float32), pltpu.SemaphoreType.DMA, pltpu.SemaphoreType.DMA],
        compiler_params=pltpu.CompilerParams(vmem_limit_bytes=2 << 20),
        name="piece",
    )(pltpu.with_memory_space_constraint(test, pltpu.HBM), pltpu.with_memory_space_constraint(deg, pltpu.HBM))


def logs_kernel(slabs, first, place, *refs):
    w_hbm, rd_hbm, row_hbm, col_hbm, samp_hbm, cnt_hbm = refs[:6]
    refs = refs[7:]
    if not first:
        _, was_s, list_s, rb_ref = refs[:4]
        refs = refs[4:]
        x_ref, cur_s, tile_s = refs[:3]
        refs = refs[3:]
    else:
        x_ref, cur_s, tile_s, rb_ref, off_s, item_s = refs[:6]
        refs = refs[6:]
    wbuf, rd_ref, row_ref, row_s, col_s, samp_s, cnt_s, sem, small, inv_s, tab_s = refs
    n_slabs, cap = w_hbm.shape[:2]
    bands, n = rb_ref.shape[:2]
    blocks = x_ref.shape[0]
    zero, trash = blocks - 2, blocks - 1
    chunks = cap // GROUP

    def copy(s, c):
        return pltpu.make_async_copy(w_hbm.at[s, pl.ds(c * GROUP, GROUP)],
                                     wbuf.at[s - slabs[0], pl.ds(c * GROUP, GROUP)], sem.at[s - slabs[0], c])

    pairs = [(cnt_hbm, cnt_s), (row_hbm, row_s), (col_hbm, col_s), (samp_hbm, samp_s)]
    if first:
        pairs += [(rd_hbm, rd_ref), (row_hbm, row_ref)]
    smalls = [pltpu.make_async_copy(p, r, small.at[i]) for i, (p, r) in enumerate(pairs)]
    for c in smalls:
        c.start()
    copy(slabs[0], 0).start()
    if first:
        x_ref[zero] = jnp.full((n, n), -1e30, jnp.float32)
    else:
        for q in range(bands):
            cur_s[q] = was_s[q]
        def keep(i, carry):
            tile_s[i] = list_s[i]
            return carry
        lax.fori_loop(0, zero, keep, 0, unroll=16)
    tile_s[zero] = 0
    for j in range(1, MOST_SAMPLES + 1):
        inv_s[j] = jnp.float32(1.0 / j)
    base, by_col, by_slab = place
    for c, v in enumerate(by_col):
        tab_s[c] = v ^ base() if base else v
    smalls[0].wait()
    for s in slabs:
        for c in range(chunks):
            if (s, c) != (slabs[0], 0):
                @pl.when(c * GROUP < cnt_s[s])
                def _():
                    copy(s, c).start()
    for c in smalls[1:]:
        c.wait()
    if first:
        for q in range(bands):
            rb_ref[q] = jnp.transpose(jnp.broadcast_to(SCALE / rd_ref[q:q + 1, :], (n, n)))
        rows = row_ref[...]
        slab = lax.broadcasted_iota(jnp.int32, rows.shape, 0)
        lane = lax.broadcasted_iota(jnp.int32, rows.shape, 1)
        live = jnp.zeros(rows.shape, jnp.int32)
        for s in range(n_slabs):
            live = jnp.where(slab == s, cnt_s[s], live)
        rows = jnp.where(lane < live, rows, bands)
        off_s[0] = 0
        cur_s[0] = 0
        for q in range(1, bands + 1):
            p = jnp.sum(jnp.where(rows < q, 1.0, 0.0)).astype(jnp.int32)
            off_s[q] = p
            if q < bands:
                cur_s[q] = p
        rounds = item_s.shape[0] // bands - 2
        starts = [off_s[q] for q in range(bands + 1)]
        count = jnp.int32(0)
        for it in range(rounds):
            for q in range(bands):
                first_at = starts[q] + it * DEPTH
                item_s[count] = q * PLACES + first_at
                count = count + (first_at < starts[q + 1]).astype(jnp.int32)
        for i in range(ITEMS[0]):
            item_s[count + i] = PLACES - 1 - DEPTH
        off_s[bands + 1] = count

    for s in slabs:
        live = cnt_s[s]
        def chunk(c, carry):
            copy(s, c).wait()
            todo = []
            for j in range(GROUP):
                k = c * GROUP + j
                ok = k < live
                q = row_s[s, k]
                p = cur_s[q]
                cur_s[q] = p + ok.astype(jnp.int32)
                dest = jnp.where(ok, p, trash)
                tile_s[dest] = tab_s[col_s[s, k]] ^ by_slab[s]
                todo.append((k, q, dest, inv_s[samp_s[s, k]]))
            for k, q, dest, sc in todo:
                x_ref[dest] = jnp.log((wbuf[s - slabs[0], k].astype(jnp.float32) * sc) * rb_ref[q])
            return carry
        lax.fori_loop(0, (live + GROUP - 1) // GROUP, chunk, 0)


def block_logs(w, rd, rows, cols, samples, counts, held, slabs, place, state=None):
    n_slabs, cap, n, _ = w.shape
    bands = rd.shape[0]
    blocks = n_slabs * cap + 2
    first = state is None
    out = [jax.ShapeDtypeStruct((blocks, n, n), jnp.float32), jax.ShapeDtypeStruct((bands,), jnp.int32),
           jax.ShapeDtypeStruct((blocks,), jnp.int32)]
    if first:
        rounds = -(-n_slabs * len(place[1]) // DEPTH)
        out += [jax.ShapeDtypeStruct((bands, n, n), jnp.float32), jax.ShapeDtypeStruct((bands + 2,), jnp.int32),
                jax.ShapeDtypeStruct(((rounds + 2) * bands,), jnp.int32)]
    HBM = pl.BlockSpec(memory_space=pltpu.HBM)
    ins = [pltpu.with_memory_space_constraint(v, pltpu.HBM) for v in (w, rd, rows, cols, samples, counts)]
    return pl.pallas_call(
        functools.partial(logs_kernel, slabs, first, place),
        out_shape=out,
        in_specs=[HBM] * 6 + [pl.BlockSpec(memory_space=pl.ANY)] + ([] if first else [VMEM, SMEM, SMEM, VMEM]),
        out_specs=[VMEM, SMEM, SMEM] + ([VMEM, SMEM, SMEM] if first else []),
        scratch_shapes=[
            pltpu.VMEM((len(slabs), cap, n, n), jnp.bfloat16),
            pltpu.VMEM((bands, n), jnp.float32),
            pltpu.VMEM(rows.shape, jnp.int32),
            pltpu.SMEM(rows.shape, jnp.int32),
            pltpu.SMEM(rows.shape, jnp.int32),
            pltpu.SMEM(rows.shape, jnp.int32),
            pltpu.SMEM(counts.shape, jnp.int32),
            pltpu.SemaphoreType.DMA((len(slabs), cap // GROUP)),
            pltpu.SemaphoreType.DMA((6,)),
            pltpu.SMEM((MOST_SAMPLES + 1,), jnp.float32),
            pltpu.SMEM((len(place[1]),), jnp.int32),
        ],
        input_output_aliases={} if first else {7: 0},
        compiler_params=pltpu.CompilerParams(vmem_limit_bytes=12 << 20),
        cost_estimate=pl.CostEstimate(flops=0, bytes_accessed=len(slabs) * cap * n * n * 4, transcendentals=0),
        name="block_logs",
    )(*ins, held, *(state[:4] if state else ()))


def products_kernel(x_ref, off_s, item_s, tile_s, *refs):
    hi_ref, lo_ref, gram_ref, g_ref, lc_ref, acc_ref = refs[-6:]
    n = x_ref.shape[-1]
    bands = off_s.shape[0] - 2
    zero = x_ref.shape[0] - 2

    at = 0
    for part in refs[:-6]:
        for i in range(part.shape[0]):
            g_ref[at] = part[i, 0:n, :]
            d = part[i, n:n + PAD, :].astype(jnp.float32)
            lc_ref[at] = jnp.broadcast_to(jnp.log(d[0:1] + d[1:2] + d[2:3]), (8, n))
            at += 1
    acc_ref[...] = jnp.zeros_like(acc_ref)

    def step(first, items):
        def run(it, carry):
            for k in range(items):
                word = item_s[first + it * items + k]
                q = word >> 16
                last = off_s[q + 1]
                e, t = [], []
                for j in range(DEPTH):
                    i = (word & (PLACES - 1)) + j
                    i = jnp.where(i < last, i, zero)
                    l = tile_s[i]
                    y = x_ref[i].reshape(n // 8, 8, n) - lc_ref[l][None]
                    e.append(jnp.maximum(y, 0.0).reshape(n, n).astype(jnp.bfloat16))
                    t.append(g_ref[l])
                acc_ref[q] += jnp.dot(jnp.concatenate(e, axis=1), jnp.concatenate(t, axis=0),
                                      preferred_element_type=jnp.float32)
            return carry
        return run
    long, short = ITEMS
    count = off_s[bands + 1]
    longs = (count + long - short - 1) // long
    lax.fori_loop(0, longs, step(0, long), 0)
    lax.fori_loop(0, (jnp.maximum(count - longs * long, 0) + short - 1) // short, step(longs * long, short), 0)

    gram = jnp.zeros((n, 2 * n), jnp.float32)
    for q in range(bands):
        a = acc_ref[q]
        h = a.astype(jnp.bfloat16)
        l = (a - h.astype(jnp.float32)).astype(jnp.bfloat16)
        hi_ref[q * n:(q + 1) * n, :] = h
        lo_ref[q * n:(q + 1) * n, :] = l
        gram = gram + lax.dot_general(h, jnp.concatenate([h, l], axis=1), (((0,), (0,)), ((), ())),
                                      preferred_element_type=jnp.float32)
    cross = gram[:, n:]
    gram_ref[...] = gram[:, :n] + (cross + jnp.transpose(cross))


def products(x, off, items, tiles, parts):
    n = x.shape[-1]
    bands = off.shape[0] - 2
    total = sum(p.shape[0] for p in parts)
    return pl.pallas_call(
        products_kernel,
        out_shape=(jax.ShapeDtypeStruct((bands * n, n), jnp.bfloat16), jax.ShapeDtypeStruct((bands * n, n), jnp.bfloat16),
                   jax.ShapeDtypeStruct((n, n), jnp.float32)),
        in_specs=[VMEM, SMEM, SMEM, SMEM] + [VMEM] * len(parts),
        out_specs=(VMEM, VMEM, VMEM),
        scratch_shapes=[
            pltpu.VMEM((total, n, n), jnp.bfloat16),
            pltpu.VMEM((total, 8, n), jnp.float32),
            pltpu.VMEM((bands, n, n), jnp.float32),
        ],
        compiler_params=pltpu.CompilerParams(vmem_limit_bytes=8 << 20),
        name="products_gram",
    )(x, off, items, tiles, *parts)


def split(x):
    h = x.astype(jnp.bfloat16)
    x = x - h.astype(jnp.float32)
    m = x.astype(jnp.bfloat16)
    return h, m, (x - m.astype(jnp.float32)).astype(jnp.bfloat16)


def stacked(x):
    h, m, l = split(x)
    return jnp.concatenate([h, h, m, m, h, l], axis=0).T, jnp.concatenate([h, m, h, m, l, h], axis=0)


def solve_kernel(nb, root, chunk, gram_ref, hi_ref, lo_ref, basis_ref, tri_ref, m_ref):
    n = gram_ref.shape[0]
    lane = lax.broadcasted_iota(jnp.int32, (1, n), 1)
    m_ref[...] = gram_ref[...]
    for r0 in range(0, n, nb):
        panel = m_ref[r0:r0 + nb, :]
        sub = lax.broadcasted_iota(jnp.int32, (nb, n), 0)
        inside = (lane >= r0) & (lane < r0 + nb)
        eye = jnp.where(lax.broadcasted_iota(jnp.int32, (nb, n), 1) == sub + r0, 1.0, 0.0)
        c = [jnp.broadcast_to(panel[:, r0 + v:r0 + v + 1], (nb, n)) for v in range(nb)]
        x = jnp.where(inside, eye, panel)
        scale = jnp.zeros((nb, n), jnp.float32)
        for t in range(nb):
            r = lax.rsqrt(c[t][t:t + 1, :])
            f = c[t] * r
            fm = jnp.where(sub > t, f, 0.0)
            for v in range(t + 1, nb):
                c[v] = c[v] - fm * f[v:v + 1, :]
            row = x[t:t + 1, :] * r
            x = jnp.where(sub == t, row, x - fm * row)
            scale = jnp.where(sub == t, r, scale)
        top = x
        for v in range(nb):
            top = jnp.where(lane == r0 + v, c[v] * scale, top)
        tri_ref[r0:r0 + nb, :] = top
        m_ref[r0:r0 + nb, :] = x
        if r0 + nb < n:
            lhs, rhs = stacked(x)
            below = jnp.where(inside, 0.0, m_ref[r0 + nb:, :])
            m_ref[r0 + nb:, :] = below - jnp.dot(lhs[r0 + nb:], rhs, preferred_element_type=jnp.float32)
    ii = lax.broadcasted_iota(jnp.int32, (n, n), 0)
    jj = lax.broadcasted_iota(jnp.int32, (n, n), 1)
    tri_ref[...] = jnp.where(jj >= ii, tri_ref[...], 0.0) * (1.0 / root)
    w = jnp.where(jj <= ii, m_ref[...], 0.0) * root
    wh = w.astype(jnp.bfloat16)
    wl = (w - wh.astype(jnp.float32)).astype(jnp.bfloat16)
    both = jnp.concatenate([wh, wl], axis=0)
    dims = (((1,), (1,)), ((), ()))
    for c in range(0, hi_ref.shape[0], chunk):
        h = hi_ref[c:c + chunk, :]
        l = lo_ref[c:c + chunk, :]
        a = lax.dot_general(h, both, dims, preferred_element_type=jnp.float32)
        b = lax.dot_general(l, wh, dims, preferred_element_type=jnp.float32)
        basis_ref[c:c + chunk, :] = a[:, :n] + (a[:, n:] + b)


def solve(gram, hi, lo, root, nb=16, chunk=256):
    n = gram.shape[0]
    V = pl.BlockSpec(memory_space=pltpu.VMEM)
    return pl.pallas_call(
        functools.partial(solve_kernel, nb, root, chunk),
        out_shape=(jax.ShapeDtypeStruct(hi.shape, jnp.float32), jax.ShapeDtypeStruct((n, n), jnp.float32)),
        in_specs=[V, V, V], out_specs=(V, V),
        scratch_shapes=[pltpu.VMEM((n, n), jnp.float32)],
        compiler_params=pltpu.CompilerParams(vmem_limit_bytes=6 << 20),
        name="cholesky_basis",
    )(gram, hi, lo)


AXES = ("rows", "blk")
STAGES = ((0, 1), (1, 2), (0, 0), (2, 4))


def send(x, mask, n_dev):
    return lax.ppermute(x, AXES, [(i, i ^ mask) for i in range(n_dev)])


def sum_all(x, n_dev):
    width = min(x.shape[1], x.size // n_dev)
    shares = x.reshape(n_dev, -1, width)
    mine = lax.all_to_all(shares, AXES, 0, 0, tiled=True).sum(axis=0)
    sent = jnp.broadcast_to(mine[None], shares.shape)
    return lax.all_to_all(sent, AXES, 0, 0, tiled=True).reshape(x.shape)


def body(block_weight, block_row, block_col, block_count, block_samples, row_degree, col_degree, test_matrix):
    n_rows, n_blk = lax.axis_size("rows"), lax.axis_size("blk")
    n_dev = n_rows * n_blk
    weights = block_weight[0, 0]
    n_slabs, _, n, _ = weights.shape
    piece_len, width = test_matrix.shape[1:]
    row_deg = row_degree[0, 0].reshape(-1, n)
    me = lax.axis_index(AXES)

    if piece_len == n:
        piece = make_piece(test_matrix[0], col_degree)
    else:
        degs = jnp.broadcast_to(jnp.pad(col_degree, ((0, 0), (0, width - piece_len)), constant_values=1.0), (PAD, width))
        rows_at = lax.broadcasted_iota(jnp.int32, degs.shape, 0)
        head = jnp.zeros_like(degs)
        for i in range(3):
            h = lax.reduce_precision(degs, 8, 7)
            head = jnp.where(rows_at == i, h, head)
            degs = degs - h
        piece = jnp.concatenate([test_matrix[0], head.astype(jnp.bfloat16)], axis=0)[None]

    bits = [1 << i for i in range(1, n_dev.bit_length() - 1)]
    line, plane = bits[2:][::-1], (bits[0], bits[1], bits[0] ^ bits[1])
    order = [0]
    for m in line:
        order = order + [v ^ m for v in order]
    order = [v ^ m for m in (0, *plane) for v in order]
    order = order + [v ^ 1 for v in order]
    n_cols = n_rows * piece_len // n
    if piece_len == n:
        weights_of = [order.index(1 << i) for i in range(n_dev.bit_length() - 1)]
        spread = lambda v: sum(w for i, w in enumerate(weights_of) if v >> i & 1)
        def base():
            at = lax.axis_index("rows") * n_blk + lax.axis_index("blk")
            return sum(((at >> i) & 1) * w for i, w in enumerate(weights_of))
        place = (base, [spread(c * n_blk) for c in range(n_cols)], [spread(s) for s in range(n_blk)])
    else:
        place = (None, [c * n_blk for c in range(n_cols)], list(range(n_blk)))
    tables = (row_deg, block_row[0, 0], block_col[0, 0], block_samples[0, 0], block_count[0, 0])
    slab_sets = [range(n_slabs * a // 4, n_slabs * b // 4) for a, b in STAGES]

    def logs(state, held, stage):
        if not len(slab_sets[stage]):
            return state
        return [*block_logs(weights, *tables, held, slab_sets[stage], place, state), *(state or [])[3:]]

    group, state = piece, None
    for step, m in enumerate(line):
        got = send(group, m, n_dev)
        stage = step - (len(line) - 2)
        if stage >= 0:
            state = logs(state, group, stage)
            if state:
                got, *state = lax.optimization_barrier((got, *state))
        group = jnp.concatenate([group, got], axis=0)
    one, two = plane[:2]
    near = send(group, two, n_dev)
    side = send(group, one, n_dev)
    swapped = send(group, 1, n_dev)
    state = logs(state, group, 2)
    near, *state = lax.optimization_barrier((near, *state))
    far = send(near, one, n_dev)
    near_swapped = send(near, 1, n_dev)
    state = logs(state, near, 3)
    side, far, swapped, near_swapped, state[0] = lax.optimization_barrier((side, far, swapped, near_swapped, state[0]))
    parts = [group, side, near, far]
    swapped = [swapped, send(side, 1, n_dev), near_swapped, send(far, 1, n_dev)]
    parts = parts + swapped
    if piece_len != n:
        share = n // piece_len
        pieces = jnp.concatenate(parts, axis=0)[jnp.argsort(me ^ jnp.asarray(order, jnp.int32))]
        pieces = pieces.reshape(n_rows // share, share, n_blk, piece_len + PAD, width).transpose(0, 2, 1, 3, 4)
        pieces = pieces.reshape(-1, share, piece_len + PAD, width)
        tiles = pieces[:, :, :piece_len].reshape(-1, n, width)
        heads = pieces[:, :, piece_len:, :piece_len].transpose(0, 2, 1, 3).reshape(-1, PAD, n)
        parts = [jnp.concatenate([tiles, heads], axis=1)]
    hi, lo, gram = products(state[0], state[4], state[5], state[2], parts)
    gram = sum_all(gram, n_dev)
    basis, triangle = solve(gram, hi, lo, math.sqrt(hi.shape[0] * n_dev))
    return basis[None, None], triangle


def solution(mesh):
    placed = (
        P("rows", "blk", None, None, None, None),
        P("rows", "blk", None, None),
        P("rows", "blk", None, None),
        P("rows", "blk", None),
        P("rows", "blk", None, None),
        P("rows", "blk", None),
        P("blk", "rows"),
        P("blk", "rows", None),
    )
    return jax.shard_map(
        body,
        mesh=mesh,
        in_specs=placed,
        out_specs=(P("rows", "blk", None, None), P()),
        check_vma=False,
    )
```

```python
import functools
import math

import jax
import jax.numpy as jnp
from jax import lax
from jax.experimental import pallas as pl
from jax.experimental.pallas import tpu as pltpu
from jax.sharding import PartitionSpec as P

SCALE = 16.0
MOST_SAMPLES = 8
GROUP = 16
DEPTH = 4
ITEMS = (32, 16)
PLACES = 1 << 16
PAD = 16
SMEM = pl.BlockSpec(memory_space=pltpu.SMEM)
VMEM = pl.BlockSpec(memory_space=pltpu.VMEM)


def piece_kernel(test_hbm, deg_hbm, out_ref, deg_ref, sem, deg_sem):
    n = test_hbm.shape[0]
    rows = pltpu.make_async_copy(test_hbm, out_ref.at[0, pl.ds(0, n)], sem)
    degs = pltpu.make_async_copy(deg_hbm, deg_ref, deg_sem)
    rows.start()
    degs.start()
    degs.wait()
    rest = jnp.broadcast_to(deg_ref[...], (PAD, deg_ref.shape[1]))
    at = lax.broadcasted_iota(jnp.int32, rest.shape, 0)
    out = jnp.zeros_like(rest)
    for i in range(3):
        h = rest.astype(jnp.bfloat16).astype(jnp.float32)
        out = jnp.where(at == i, h, out)
        rest = rest - h
    out_ref[0, n:n + PAD, :] = out.astype(jnp.bfloat16)
    rows.wait()


def make_piece(test, deg):
    n, width = test.shape
    HBM = pl.BlockSpec(memory_space=pltpu.HBM)
    return pl.pallas_call(
        piece_kernel,
        out_shape=jax.ShapeDtypeStruct((1, n + PAD, width), jnp.bfloat16),
        in_specs=[HBM, HBM],
        out_specs=VMEM,
        scratch_shapes=[pltpu.VMEM((1, width), jnp.float32), pltpu.SemaphoreType.DMA, pltpu.SemaphoreType.DMA],
        compiler_params=pltpu.CompilerParams(vmem_limit_bytes=2 << 20),
        name="piece",
    )(pltpu.with_memory_space_constraint(test, pltpu.HBM), pltpu.with_memory_space_constraint(deg, pltpu.HBM))


def logs_kernel(slabs, first, place, *refs):
    w_hbm, rd_hbm, row_hbm, col_hbm, samp_hbm, cnt_hbm = refs[:6]
    refs = refs[7:]
    if not first:
        _, was_s, list_s, rb_ref = refs[:4]
        refs = refs[4:]
        x_ref, cur_s, tile_s = refs[:3]
        refs = refs[3:]
    else:
        x_ref, cur_s, tile_s, rb_ref, off_s, item_s = refs[:6]
        refs = refs[6:]
    wbuf, rd_ref, row_ref, row_s, col_s, samp_s, cnt_s, sem, small, inv_s, tab_s = refs
    n_slabs, cap = w_hbm.shape[:2]
    bands, n = rb_ref.shape[:2]
    blocks = x_ref.shape[0]
    zero, trash = blocks - 2, blocks - 1
    chunks = cap // GROUP

    def copy(s, c):
        return pltpu.make_async_copy(w_hbm.at[s, pl.ds(c * GROUP, GROUP)],
                                     wbuf.at[s - slabs[0], pl.ds(c * GROUP, GROUP)], sem.at[s - slabs[0], c])

    pairs = [(cnt_hbm, cnt_s), (row_hbm, row_s), (col_hbm, col_s), (samp_hbm, samp_s)]
    if first:
        pairs += [(rd_hbm, rd_ref), (row_hbm, row_ref)]
    smalls = [pltpu.make_async_copy(p, r, small.at[i]) for i, (p, r) in enumerate(pairs)]
    for c in smalls:
        c.start()
    copy(slabs[0], 0).start()
    if first:
        x_ref[zero] = jnp.full((n, n), -1e30, jnp.float32)
    else:
        for q in range(bands):
            cur_s[q] = was_s[q]
        def keep(i, carry):
            tile_s[i] = list_s[i]
            return carry
        lax.fori_loop(0, zero, keep, 0, unroll=16)
    tile_s[zero] = 0
    for j in range(1, MOST_SAMPLES + 1):
        inv_s[j] = jnp.float32(1.0 / j)
    base, by_col, by_slab = place
    for c, v in enumerate(by_col):
        tab_s[c] = v ^ base() if base else v
    smalls[0].wait()
    for s in slabs:
        for c in range(chunks):
            if (s, c) != (slabs[0], 0):
                @pl.when(c * GROUP < cnt_s[s])
                def _():
                    copy(s, c).start()
    for c in smalls[1:]:
        c.wait()
    if first:
        for q in range(bands):
            rb_ref[q] = jnp.transpose(jnp.broadcast_to(SCALE / rd_ref[q:q + 1, :], (n, n)))
        rows = row_ref[...]
        slab = lax.broadcasted_iota(jnp.int32, rows.shape, 0)
        lane = lax.broadcasted_iota(jnp.int32, rows.shape, 1)
        live = jnp.zeros(rows.shape, jnp.int32)
        for s in range(n_slabs):
            live = jnp.where(slab == s, cnt_s[s], live)
        rows = jnp.where(lane < live, rows, bands)
        off_s[0] = 0
        cur_s[0] = 0
        for q in range(1, bands + 1):
            p = jnp.sum(jnp.where(rows < q, 1.0, 0.0)).astype(jnp.int32)
            off_s[q] = p
            if q < bands:
                cur_s[q] = p
        rounds = item_s.shape[0] // bands - 2
        starts = [off_s[q] for q in range(bands + 1)]
        count = jnp.int32(0)
        for it in range(rounds):
            for q in range(bands):
                first_at = starts[q] + it * DEPTH
                item_s[count] = q * PLACES + first_at
                count = count + (first_at < starts[q + 1]).astype(jnp.int32)
        for i in range(ITEMS[0]):
            item_s[count + i] = PLACES - 1 - DEPTH
        off_s[bands + 1] = count

    for s in slabs:
        live = cnt_s[s]
        def chunk(c, carry):
            copy(s, c).wait()
            todo = []
            for j in range(GROUP):
                k = c * GROUP + j
                ok = k < live
                q = row_s[s, k]
                p = cur_s[q]
                cur_s[q] = p + ok.astype(jnp.int32)
                dest = jnp.where(ok, p, trash)
                tile_s[dest] = tab_s[col_s[s, k]] ^ by_slab[s]
                todo.append((k, q, dest, inv_s[samp_s[s, k]]))
            for k, q, dest, sc in todo:
                x_ref[dest] = jnp.log((wbuf[s - slabs[0], k].astype(jnp.float32) * sc) * rb_ref[q])
            return carry
        lax.fori_loop(0, (live + GROUP - 1) // GROUP, chunk, 0)


def block_logs(w, rd, rows, cols, samples, counts, held, slabs, place, state=None):
    n_slabs, cap, n, _ = w.shape
    bands = rd.shape[0]
    blocks = n_slabs * cap + 2
    first = state is None
    out = [jax.ShapeDtypeStruct((blocks, n, n), jnp.float32), jax.ShapeDtypeStruct((bands,), jnp.int32),
           jax.ShapeDtypeStruct((blocks,), jnp.int32)]
    if first:
        rounds = -(-n_slabs * len(place[1]) // DEPTH)
        out += [jax.ShapeDtypeStruct((bands, n, n), jnp.float32), jax.ShapeDtypeStruct((bands + 2,), jnp.int32),
                jax.ShapeDtypeStruct(((rounds + 2) * bands,), jnp.int32)]
    HBM = pl.BlockSpec(memory_space=pltpu.HBM)
    ins = [pltpu.with_memory_space_constraint(v, pltpu.HBM) for v in (w, rd, rows, cols, samples, counts)]
    return pl.pallas_call(
        functools.partial(logs_kernel, slabs, first, place),
        out_shape=out,
        in_specs=[HBM] * 6 + [pl.BlockSpec(memory_space=pl.ANY)] + ([] if first else [VMEM, SMEM, SMEM, VMEM]),
        out_specs=[VMEM, SMEM, SMEM] + ([VMEM, SMEM, SMEM] if first else []),
        scratch_shapes=[
            pltpu.VMEM((len(slabs), cap, n, n), jnp.bfloat16),
            pltpu.VMEM((bands, n), jnp.float32),
            pltpu.VMEM(rows.shape, jnp.int32),
            pltpu.SMEM(rows.shape, jnp.int32),
            pltpu.SMEM(rows.shape, jnp.int32),
            pltpu.SMEM(rows.shape, jnp.int32),
            pltpu.SMEM(counts.shape, jnp.int32),
            pltpu.SemaphoreType.DMA((len(slabs), cap // GROUP)),
            pltpu.SemaphoreType.DMA((6,)),
            pltpu.SMEM((MOST_SAMPLES + 1,), jnp.float32),
            pltpu.SMEM((len(place[1]),), jnp.int32),
        ],
        input_output_aliases={} if first else {7: 0},
        compiler_params=pltpu.CompilerParams(vmem_limit_bytes=12 << 20),
        cost_estimate=pl.CostEstimate(flops=0, bytes_accessed=len(slabs) * cap * n * n * 4, transcendentals=0),
        name="block_logs",
    )(*ins, held, *(state[:4] if state else ()))


def products_kernel(x_ref, off_s, item_s, tile_s, *refs):
    hi_ref, lo_ref, gram_ref, g_ref, lc_ref, acc_ref = refs[-6:]
    n = x_ref.shape[-1]
    bands = off_s.shape[0] - 2
    zero = x_ref.shape[0] - 2

    at = 0
    for part in refs[:-6]:
        for i in range(part.shape[0]):
            g_ref[at] = part[i, 0:n, :]
            d = part[i, n:n + PAD, :].astype(jnp.float32)
            lc_ref[at] = jnp.broadcast_to(jnp.log(d[0:1] + d[1:2] + d[2:3]), (8, n))
            at += 1
    acc_ref[...] = jnp.zeros_like(acc_ref)

    def step(first, items):
        def run(it, carry):
            for k in range(items):
                word = item_s[first + it * items + k]
                q = word >> 16
                last = off_s[q + 1]
                e, t = [], []
                for j in range(DEPTH):
                    i = (word & (PLACES - 1)) + j
                    i = jnp.where(i < last, i, zero)
                    l = tile_s[i]
                    y = x_ref[i].reshape(n // 8, 8, n) - lc_ref[l][None]
                    e.append(jnp.maximum(y, 0.0).reshape(n, n).astype(jnp.bfloat16))
                    t.append(g_ref[l])
                acc_ref[q] += jnp.dot(jnp.concatenate(e, axis=1), jnp.concatenate(t, axis=0),
                                      preferred_element_type=jnp.float32)
            return carry
        return run
    long, short = ITEMS
    count = off_s[bands + 1]
    longs = (count + long - short - 1) // long
    lax.fori_loop(0, longs, step(0, long), 0)
    lax.fori_loop(0, (jnp.maximum(count - longs * long, 0) + short - 1) // short, step(longs * long, short), 0)

    gram = jnp.zeros((n, 2 * n), jnp.float32)
    for q in range(bands):
        a = acc_ref[q]
        h = a.astype(jnp.bfloat16)
        l = (a - h.astype(jnp.float32)).astype(jnp.bfloat16)
        hi_ref[q * n:(q + 1) * n, :] = h
        lo_ref[q * n:(q + 1) * n, :] = l
        gram = gram + lax.dot_general(h, jnp.concatenate([h, l], axis=1), (((0,), (0,)), ((), ())),
                                      preferred_element_type=jnp.float32)
    cross = gram[:, n:]
    gram_ref[...] = gram[:, :n] + (cross + jnp.transpose(cross))


def products(x, off, items, tiles, parts):
    n = x.shape[-1]
    bands = off.shape[0] - 2
    total = sum(p.shape[0] for p in parts)
    return pl.pallas_call(
        products_kernel,
        out_shape=(jax.ShapeDtypeStruct((bands * n, n), jnp.bfloat16), jax.ShapeDtypeStruct((bands * n, n), jnp.bfloat16),
                   jax.ShapeDtypeStruct((n, n), jnp.float32)),
        in_specs=[VMEM, SMEM, SMEM, SMEM] + [VMEM] * len(parts),
        out_specs=(VMEM, VMEM, VMEM),
        scratch_shapes=[
            pltpu.VMEM((total, n, n), jnp.bfloat16),
            pltpu.VMEM((total, 8, n), jnp.float32),
            pltpu.VMEM((bands, n, n), jnp.float32),
        ],
        compiler_params=pltpu.CompilerParams(vmem_limit_bytes=8 << 20),
        name="products_gram",
    )(x, off, items, tiles, *parts)


def split(x):
    h = x.astype(jnp.bfloat16)
    x = x - h.astype(jnp.float32)
    m = x.astype(jnp.bfloat16)
    return h, m, (x - m.astype(jnp.float32)).astype(jnp.bfloat16)


def stacked(x):
    h, m, l = split(x)
    return jnp.concatenate([h, h, m, m, h, l], axis=0).T, jnp.concatenate([h, m, h, m, l, h], axis=0)


def solve_kernel(nb, root, chunk, gram_ref, hi_ref, lo_ref, basis_ref, tri_ref, m_ref):
    n = gram_ref.shape[0]
    lane = lax.broadcasted_iota(jnp.int32, (1, n), 1)
    m_ref[...] = gram_ref[...]
    for r0 in range(0, n, nb):
        panel = m_ref[r0:r0 + nb, :]
        sub = lax.broadcasted_iota(jnp.int32, (nb, n), 0)
        inside = (lane >= r0) & (lane < r0 + nb)
        eye = jnp.where(lax.broadcasted_iota(jnp.int32, (nb, n), 1) == sub + r0, 1.0, 0.0)
        c = [jnp.broadcast_to(panel[:, r0 + v:r0 + v + 1], (nb, n)) for v in range(nb)]
        x = jnp.where(inside, eye, panel)
        scale = jnp.zeros((nb, n), jnp.float32)
        for t in range(nb):
            r = lax.rsqrt(c[t][t:t + 1, :])
            f = c[t] * r
            fm = jnp.where(sub > t, f, 0.0)
            for v in range(t + 1, nb):
                c[v] = c[v] - fm * f[v:v + 1, :]
            row = x[t:t + 1, :] * r
            x = jnp.where(sub == t, row, x - fm * row)
            scale = jnp.where(sub == t, r, scale)
        top = x
        for v in range(nb):
            top = jnp.where(lane == r0 + v, c[v] * scale, top)
        tri_ref[r0:r0 + nb, :] = top
        m_ref[r0:r0 + nb, :] = x
        if r0 + nb < n:
            lhs, rhs = stacked(x)
            below = jnp.where(inside, 0.0, m_ref[r0 + nb:, :])
            m_ref[r0 + nb:, :] = below - jnp.dot(lhs[r0 + nb:], rhs, preferred_element_type=jnp.float32)
    ii = lax.broadcasted_iota(jnp.int32, (n, n), 0)
    jj = lax.broadcasted_iota(jnp.int32, (n, n), 1)
    tri_ref[...] = jnp.where(jj >= ii, tri_ref[...], 0.0) * (1.0 / root)
    w = jnp.where(jj <= ii, m_ref[...], 0.0) * root
    wh = w.astype(jnp.bfloat16)
    wl = (w - wh.astype(jnp.float32)).astype(jnp.bfloat16)
    both = jnp.concatenate([wh, wl], axis=0)
    dims = (((1,), (1,)), ((), ()))
    for c in range(0, hi_ref.shape[0], chunk):
        h = hi_ref[c:c + chunk, :]
        l = lo_ref[c:c + chunk, :]
        a = lax.dot_general(h, both, dims, preferred_element_type=jnp.float32)
        b = lax.dot_general(l, wh, dims, preferred_element_type=jnp.float32)
        basis_ref[c:c + chunk, :] = a[:, :n] + (a[:, n:] + b)


def solve(gram, hi, lo, root, nb=16, chunk=256):
    n = gram.shape[0]
    V = pl.BlockSpec(memory_space=pltpu.VMEM)
    return pl.pallas_call(
        functools.partial(solve_kernel, nb, root, chunk),
        out_shape=(jax.ShapeDtypeStruct(hi.shape, jnp.float32), jax.ShapeDtypeStruct((n, n), jnp.float32)),
        in_specs=[V, V, V], out_specs=(V, V),
        scratch_shapes=[pltpu.VMEM((n, n), jnp.float32)],
        compiler_params=pltpu.CompilerParams(vmem_limit_bytes=6 << 20),
        name="cholesky_basis",
    )(gram, hi, lo)


AXES = ("rows", "blk")
STAGES = ((0, 2), (2, 3), (0, 0), (3, 4))


def send(x, mask, n_dev):
    return lax.ppermute(x, AXES, [(i, i ^ mask) for i in range(n_dev)])


def sum_all(x, n_dev):
    width = min(x.shape[1], x.size // n_dev)
    shares = x.reshape(n_dev, -1, width)
    mine = lax.all_to_all(shares, AXES, 0, 0, tiled=True).sum(axis=0)
    sent = jnp.broadcast_to(mine[None], shares.shape)
    return lax.all_to_all(sent, AXES, 0, 0, tiled=True).reshape(x.shape)


def body(block_weight, block_row, block_col, block_count, block_samples, row_degree, col_degree, test_matrix):
    n_rows, n_blk = lax.axis_size("rows"), lax.axis_size("blk")
    n_dev = n_rows * n_blk
    weights = block_weight[0, 0]
    n_slabs, _, n, _ = weights.shape
    piece_len, width = test_matrix.shape[1:]
    row_deg = row_degree[0, 0].reshape(-1, n)
    me = lax.axis_index(AXES)

    if piece_len == n:
        piece = make_piece(test_matrix[0], col_degree)
    else:
        degs = jnp.broadcast_to(jnp.pad(col_degree, ((0, 0), (0, width - piece_len)), constant_values=1.0), (PAD, width))
        rows_at = lax.broadcasted_iota(jnp.int32, degs.shape, 0)
        head = jnp.zeros_like(degs)
        for i in range(3):
            h = lax.reduce_precision(degs, 8, 7)
            head = jnp.where(rows_at == i, h, head)
            degs = degs - h
        piece = jnp.concatenate([test_matrix[0], head.astype(jnp.bfloat16)], axis=0)[None]

    bits = [1 << i for i in range(1, n_dev.bit_length() - 1)]
    line, plane = bits[2:][::-1], (bits[0], bits[1], bits[0] ^ bits[1])
    order = [0]
    for m in line:
        order = order + [v ^ m for v in order]
    order = [v ^ m for m in (0, *plane) for v in order]
    order = order + [v ^ 1 for v in order]
    n_cols = n_rows * piece_len // n
    if piece_len == n:
        weights_of = [order.index(1 << i) for i in range(n_dev.bit_length() - 1)]
        spread = lambda v: sum(w for i, w in enumerate(weights_of) if v >> i & 1)
        def base():
            at = lax.axis_index("rows") * n_blk + lax.axis_index("blk")
            return sum(((at >> i) & 1) * w for i, w in enumerate(weights_of))
        place = (base, [spread(c * n_blk) for c in range(n_cols)], [spread(s) for s in range(n_blk)])
    else:
        place = (None, [c * n_blk for c in range(n_cols)], list(range(n_blk)))
    tables = (row_deg, block_row[0, 0], block_col[0, 0], block_samples[0, 0], block_count[0, 0])
    slab_sets = [range(n_slabs * a // 4, n_slabs * b // 4) for a, b in STAGES]

    def logs(state, held, stage):
        if not len(slab_sets[stage]):
            return state
        return [*block_logs(weights, *tables, held, slab_sets[stage], place, state), *(state or [])[3:]]

    group, state = piece, None
    for step, m in enumerate(line):
        got = send(group, m, n_dev)
        stage = step - (len(line) - 2)
        if stage >= 0:
            state = logs(state, group, stage)
            if state:
                got, *state = lax.optimization_barrier((got, *state))
        group = jnp.concatenate([group, got], axis=0)
    one, two = plane[:2]
    near = send(group, two, n_dev)
    side = send(group, one, n_dev)
    swapped = send(group, 1, n_dev)
    state = logs(state, group, 2)
    near, *state = lax.optimization_barrier((near, *state))
    far = send(near, one, n_dev)
    near_swapped = send(near, 1, n_dev)
    state = logs(state, near, 3)
    side, far, swapped, near_swapped, state[0] = lax.optimization_barrier((side, far, swapped, near_swapped, state[0]))
    parts = [group, side, near, far]
    swapped = [swapped, send(side, 1, n_dev), near_swapped, send(far, 1, n_dev)]
    parts = parts + swapped
    if piece_len != n:
        share = n // piece_len
        pieces = jnp.concatenate(parts, axis=0)[jnp.argsort(me ^ jnp.asarray(order, jnp.int32))]
        pieces = pieces.reshape(n_rows // share, share, n_blk, piece_len + PAD, width).transpose(0, 2, 1, 3, 4)
        pieces = pieces.reshape(-1, share, piece_len + PAD, width)
        tiles = pieces[:, :, :piece_len].reshape(-1, n, width)
        heads = pieces[:, :, piece_len:, :piece_len].transpose(0, 2, 1, 3).reshape(-1, PAD, n)
        parts = [jnp.concatenate([tiles, heads], axis=1)]
    hi, lo, gram = products(state[0], state[4], state[5], state[2], parts)
    gram = sum_all(gram, n_dev)
    basis, triangle = solve(gram, hi, lo, math.sqrt(hi.shape[0] * n_dev))
    return basis[None, None], triangle


def solution(mesh):
    placed = (
        P("rows", "blk", None, None, None, None),
        P("rows", "blk", None, None),
        P("rows", "blk", None, None),
        P("rows", "blk", None),
        P("rows", "blk", None, None),
        P("rows", "blk", None),
        P("blk", "rows"),
        P("blk", "rows", None),
    )
    return jax.shard_map(
        body,
        mesh=mesh,
        in_specs=placed,
        out_specs=(P("rows", "blk", None, None), P()),
        check_vma=False,
    )
```
